32 devices in a mesh: tm: 4 (over x, core), space: 8 (over z, y).
Axes of the slice: x: 2, y: 2, z: 4, core: 2. Of those that a mesh axis runs over, the one named last changes fastest.
Arguments:
- latent_tokens: bfloat16 [16, 8, 64, 64], P('tm', None, 'space'), may hold values from -12 to 12
- conv_in_weight: bfloat16 [3, 3, 3, 16, 384], replicated, may hold values from -0.3125 to 0.3125
- conv_in_bias: float32 [384], replicated, may hold values from -3 to 3
- norm_gain: float32 [384], replicated, may hold values from 0.25 to 1.75
- conv_mid_weight: bfloat16 [3, 3, 3, 384, 384], replicated, may hold values from -0.0625 to 0.0625
- conv_mid_bias: float32 [384], replicated, may hold values from -3 to 3
Outputs:
- decoded: bfloat16 [16, 16, 128, 384], P('tm', 'space')
The draws below stay inside these ranges and needn't reach their ends.
All inputs are finite; a program needn't handle non-finite values.
Results may differ from the reference program's by a relative error of at most 0.005.
Values may be sent and summed in bfloat16 or wider, within the bound.
No kernel may reach another device: no remote copies, remote signals or barrier semaphores. Data moves between devices by JAX's collectives and lax.ppermute only.
A program may use at most 128 MiB of HBM per device.

```python
import math
import jax
import jax.numpy as jnp
from jax import lax

ZCH = 16
CMID = 384
TW = 64
FRAMES = 16
TH = 8


def draw_latent_tokens(key, part):
    shape = (FRAMES, TH, TW, 4, ZCH)
    scales = jnp.exp(jax.random.uniform(jax.random.fold_in(key, 301), (FRAMES, TH, TW, 4, 1), jnp.float32, math.log(0.3), math.log(3.0)))
    base = jnp.clip(jax.random.normal(jax.random.fold_in(key, 303), shape, jnp.float32), -4.0, 4.0)
    return (base * scales).reshape(FRAMES, TH, TW, 4 * ZCH).astype(jnp.bfloat16)


def scatter_about(own_key, shape, scale, limit, kind=jnp.bfloat16):
    array = jax.random.normal(own_key, shape, jnp.float32) * scale
    return jnp.minimum(jnp.maximum(array, -limit), limit).astype(kind)


def setup_inputs(seed: int = 0) -> dict:
    splits = jax.random.split(jax.random.key(seed), 7)
    latent_tokens = draw_latent_tokens(jax.random.fold_in(splits[6], 71), 0)
    conv_in_weight = scatter_about(splits[1], (3, 3, 3, ZCH, CMID), (27 * ZCH) ** -0.5, 0.3125)
    conv_in_bias = scatter_about(splits[2], (CMID,), 0.5, 3.0, jnp.float32)
    norm_gain = jnp.clip(1.0 + 0.15 * jax.random.normal(splits[3], (CMID,), jnp.float32), 0.25, 1.75)
    conv_mid_weight = scatter_about(splits[4], (3, 3, 3, CMID, CMID), (27 * CMID) ** -0.5, 0.0625)
    conv_mid_bias = scatter_about(splits[5], (CMID,), 0.5, 3.0, jnp.float32)
    return {"latent_tokens": latent_tokens, "conv_in_weight": conv_in_weight, "conv_in_bias": conv_in_bias, "norm_gain": norm_gain, "conv_mid_weight": conv_mid_weight, "conv_mid_bias": conv_mid_bias}


def causal_conv(padded, weight):
    frames = padded.shape[0] - 2
    height = padded.shape[1] - 2
    breadth = padded.shape[2] - 2
    summed = jnp.zeros((frames * height * breadth, weight.shape[-1]), jnp.float32)
    for tap_time in range(3):
        for tap_row in range(3):
            for tap_col in range(3):
                window = padded[tap_time:tap_time + frames, tap_row:tap_row + height, tap_col:tap_col + breadth]
                summed = summed + jnp.dot(window.reshape(-1, window.shape[-1]), weight[tap_time, tap_row, tap_col], preferred_element_type=jnp.float32)
    return summed.reshape(frames, height, breadth, weight.shape[-1])

def unpatch(tokens):
    frames, height, breadth, _ = tokens.shape
    grid = tokens.reshape(frames, height, breadth, 2, 2, -1).transpose(0, 1, 3, 2, 4, 5)
    return grid.reshape(frames, 2 * height, 2 * breadth, -1)

def activate(feature, norm_gain):
    values = feature.astype(jnp.float32)
    spread = jnp.sqrt(lax.optimization_barrier(jnp.mean(values * values, axis=-1, keepdims=True)) + 1e-06)
    return jax.nn.silu(values / spread * norm_gain).astype(jnp.bfloat16)

def framewise(source, weight):
    padded = jnp.pad(source, ((2, 0), (1, 1), (1, 1), (0, 0)))

    def one_frame(start):
        window = lax.dynamic_slice_in_dim(padded, start, 3, 0)
        return causal_conv(window, weight)[0]
    return lax.map(one_frame, jnp.arange(source.shape[0], dtype=jnp.int32))

def reference(latent_tokens, conv_in_weight, conv_in_bias, norm_gain, conv_mid_weight, conv_mid_bias):
    latents = unpatch(latent_tokens)
    feature = (framewise(latents, conv_in_weight) + conv_in_bias).astype(jnp.bfloat16)
    activated = activate(feature, norm_gain)
    mixed_sum = framewise(activated, conv_mid_weight)
    decoded = (feature.astype(jnp.float32) + mixed_sum + conv_mid_bias).astype(jnp.bfloat16)
    return decoded
```

```python
import functools

import jax
import jax.numpy as jnp
from jax import lax
from jax.experimental import pallas as pl
from jax.experimental.pallas import tpu as pltpu
from jax.sharding import PartitionSpec as P

BF16 = jnp.bfloat16
F32 = jnp.float32
LANES = 128


def dot(left, right):
    return jnp.dot(left, right, preferred_element_type=F32)


def moved_down(value):
    row = lax.broadcasted_iota(jnp.int32, value.shape, 0)
    return jnp.where(row == 0, 0.0, pltpu.roll(value, 1, 0))


def moved_up(value):
    rows = value.shape[0]
    row = lax.broadcasted_iota(jnp.int32, value.shape, 0)
    return jnp.where(row == rows - 1, 0.0, pltpu.roll(value, rows - 1, 0))


def position():
    return lax.axis_index("space")


def chunks_kernel(own_ref, keep_ref, send_ref):
    frames, rows, cols, width = own_ref.shape
    bits = rows.bit_length() - 1
    me = position()
    for relative in range(rows):
        to = [relative >> bit & 1 for bit in range(bits)]
        out_ref = send_ref if to[0] else keep_ref
        tile = me ^ relative
        for near in range(3):
            row = tile + near - 1
            inside = jnp.logical_and(row >= 0, row < rows)
            value = own_ref[:, jnp.clip(row, 0, rows - 1)]
            value = jnp.where(inside, value, jnp.zeros_like(value))
            for pair in range(frames // 2):
                out_ref[(*to[1:], near, pair)] = jnp.concatenate(
                    [value[2 * pair], value[2 * pair + 1]], -1
                )


def token_weight_kernel(conv_in_ref, token_weight_ref):
    ch = conv_in_ref.shape[3]
    mid = conv_in_ref.shape[4]
    token_weight_ref[...] = jnp.zeros_like(token_weight_ref)
    for time in range(3):
        for parity in range(2):
            for near in range(2):
                for b in range(3):
                    for e in range(3):
                        row = near + b
                        col = e + 1 - parity
                        at = (((col // 2) * 2 + row // 2) * 2 + row % 2) * 2 + col % 2
                        token_weight_ref[
                            parity, time, at * ch : (at + 1) * ch, near * mid : (near + 1) * mid
                        ] = conv_in_ref[time, b, e]


def mixed_kernel(time, conv_mid_ref, mixed_ref, taps, arrived):
    mid = conv_mid_ref.shape[-1]
    parts = arrived.shape[0]
    size = mid // parts
    step = 16

    def spread(g0, g1, g2):
        ends = g0 + g2
        return g0, ends + g1, ends - g1, g2

    def one(i, carry):
        at = pl.ds(pl.multiple_of(i * step, step), step)
        cols = [
            spread(*[taps[b, e, at, :].astype(F32) for b in range(3)]) for e in range(3)
        ]
        for u in range(4):
            for v, value in enumerate(spread(*[cols[e][u] for e in range(3)])):
                mixed_ref[u * 4 + v, at, :] = value.astype(BF16)
        return carry

    copies = []
    for part in range(parts):
        at = pl.ds(part * size, size)
        copies.append(
            pltpu.make_async_copy(
                conv_mid_ref.at[time, :, :, at], taps.at[:, :, at], arrived.at[part]
            )
        )
        copies[-1].start()
    for part in range(parts):
        copies[part].wait()
        lax.fori_loop(part * size // step, (part + 1) * size // step, one, 0)


def block_kernel(
    previous_ref,
    own_ref,
    token_weight_ref,
    in_bias_ref,
    gain_ref,
    mixed_0_ref,
    mixed_1_ref,
    mixed_2_ref,
    mid_bias_ref,
    out_ref,
    windows,
    active,
    feature,
    spectrum,
    lines,
):
    tiles, _, pairs, cols, pair = own_ref.shape
    wide = tiles * cols
    frames, rows, _, mid = out_ref.shape
    grown = frames + 2
    width = pair // 2
    me = position()

    with jax.named_scope("windows"):
        for part, ref in enumerate((previous_ref, own_ref)):
            got = [ref[tile ^ me].astype(F32) for tile in range(tiles)]
            for two in range(pairs):
                line = [
                    jnp.concatenate([value[near, two] for value in got], 0) for near in range(3)
                ]
                for half in range(2):
                    above, below = line[half], line[half + 1]
                    for odd in range(2):
                        f = 2 * (part * pairs + two) + odd
                        at = slice(odd * width, (odd + 1) * width)
                        value = jnp.concatenate([above[:, at], below[:, at]], -1)
                        here = value.astype(BF16)
                        windows[0, half, f] = jnp.concatenate(
                            [moved_down(value).astype(BF16), here], -1
                        )
                        windows[1, half, f] = jnp.concatenate(
                            [here, moved_up(value).astype(BF16)], -1
                        )

    in_bias = in_bias_ref[...].reshape(1, mid)
    half_gain = gain_ref[...].reshape(1, mid) * 0.5
    first = (lax.axis_index("tm") > 0).astype(F32)
    top = (me > 0).astype(F32)
    bottom = (me < tiles - 1).astype(F32)
    with jax.named_scope("features"):
        for parity in range(2):
            weight = token_weight_ref[parity].reshape(6 * pair, 2 * mid)
            for half in range(2):
                left = jnp.concatenate(
                    [
                        windows[parity, half, a : a + grown].reshape(grown * wide, 2 * pair)
                        for a in range(3)
                    ],
                    -1,
                )
                summed = dot(left, weight)
                for near in range(2):
                    row = half * 2 + near
                    rounded = (summed[:, near * mid : (near + 1) * mid] + in_bias).astype(BF16)
                    if row in (1, 2):
                        feature[row - 1, parity] = rounded[2 * wide :].reshape(frames, wide, mid)
                    value = rounded.astype(F32)
                    mean = jnp.mean(value * value, axis=-1, keepdims=True)
                    scale = lax.rsqrt(mean + 1e-06)
                    if row == 0:
                        scale = scale * top
                    if row == 3:
                        scale = scale * bottom
                    scale = jnp.concatenate([scale[: 2 * wide] * first, scale[2 * wide :]], 0)
                    h = value * scale * half_gain
                    active[row, parity] = (h + h * jnp.tanh(h)).astype(BF16).reshape(grown, wide, mid)

    with jax.named_scope("spectrum"):

        def one_frame(f, carry):
            cells = []
            for row in range(4):
                even = active[row, 0, f].astype(F32)
                odd = active[row, 1, f].astype(F32)
                cells.append(
                    (moved_down(odd) - odd, even + odd, odd - even, even - moved_up(even))
                )
            for v in range(4):
                r0, r1, r2, r3 = [cells[row][v] for row in range(4)]
                spectrum[v, f] = (r0 - r2).astype(BF16)
                spectrum[4 + v, f] = (r1 + r2).astype(BF16)
                spectrum[8 + v, f] = (r2 - r1).astype(BF16)
                spectrum[12 + v, f] = (r1 - r3).astype(BF16)
            return carry

        lax.fori_loop(0, grown, one_frame, 0)

    def back(m0, m1, m2, m3):
        return m0 + 0.5 * (m1 + m2), 0.5 * (m1 - m2) - m3

    with jax.named_scope("mix"):
        mixed = (mixed_0_ref, mixed_1_ref, mixed_2_ref)
        sums = []
        for u in range(4):
            parts = []
            for v in range(4):
                at = u * 4 + v
                left = jnp.concatenate(
                    [
                        spectrum[at, a : a + frames].reshape(frames * wide, mid)
                        for a in range(3)
                    ],
                    -1,
                )
                right = jnp.concatenate([ref[at] for ref in mixed], 0)
                parts.append(dot(left, right))
            sums.append(back(*parts))
        mid_bias = mid_bias_ref[...].reshape(1, mid)
        for parity in range(2):
            for row, total in enumerate(back(*[sums[u][parity] for u in range(4)])):
                total = (total + mid_bias).reshape(frames, wide, mid)
                total = total + feature[row, parity].astype(F32)
                for f in range(frames):
                    for lane in range(mid // LANES):
                        lines[f, row, lane, pl.ds(parity, wide, stride=2), :] = total[
                            f, :, lane * LANES : (lane + 1) * LANES
                        ]
        for f in range(frames):
            for row in range(rows):
                for lane in range(mid // LANES):
                    out_ref[f, row, :, lane * LANES : (lane + 1) * LANES] = lines[
                        f, row, lane
                    ].astype(BF16)


def limited(mebibytes):
    return pltpu.CompilerParams(vmem_limit_bytes=mebibytes * 2**20)


def after(value, *others):
    return lax.optimization_barrier((value, *others))[0]


def exchanged(keep, send, axis, beside):
    count = lax.axis_size(axis)
    keep, send = keep[None], send[None]
    bit = 1
    while True:
        got = lax.ppermute(send, axis, [(at, at ^ bit) for at in range(count)])
        done = beside(send)
        held = jnp.concatenate([keep, got], 0)
        bit *= 2
        if bit == count:
            return after(held, *done)
        keep, send = held[:, 0], after(held[:, 1], *done)


def shifted(value, axis):
    count = lax.axis_size(axis)
    return lax.ppermute(value, axis, [(at, at + 1) for at in range(count - 1)])


def per_device(
    latent_tokens, conv_in_weight, conv_in_bias, norm_gain, conv_mid_weight, conv_mid_bias
):
    frames, token_rows, cols, width = latent_tokens.shape
    tiles = lax.axis_size("space")
    assert token_rows == tiles and tiles & (tiles - 1) == 0 and frames == 4
    mid = conv_mid_weight.shape[-1]
    wide = tiles * cols
    grown = frames + 2
    line = (3, frames // 2, cols, 2 * width)

    bits = tiles.bit_length() - 1
    half = jax.ShapeDtypeStruct((2,) * (bits - 1) + line, BF16)
    keep, send = pl.pallas_call(chunks_kernel, out_shape=(half, half), compiler_params=limited(2), name="chunks")(
        latent_tokens
    )
    mixed = []

    def beside(value):
        time = len(mixed)
        if time == 3:
            return ()
        mixed.append(
            pl.pallas_call(
                functools.partial(mixed_kernel, time),
                out_shape=pltpu.VMEM((16, mid, mid), BF16),
                in_specs=[pl.BlockSpec(memory_space=pltpu.HBM)],
                scratch_shapes=[
                    pltpu.VMEM((3, 3, mid, mid), BF16),
                    pltpu.SemaphoreType.DMA((4,)),
                ],
                cost_estimate=pl.CostEstimate(
                    flops=0, bytes_accessed=50 * mid * mid, transcendentals=0
                ),
                compiler_params=limited(6),
                name="mixed",
            )(pltpu.with_memory_space_constraint(after(conv_mid_weight, value), pltpu.HBM))
        )
        return mixed[-1:]

    own = exchanged(keep, send, "space", beside)
    while len(mixed) < 3:
        beside(own)
    previous = shifted(own, "tm")
    token_weight = pl.pallas_call(
        token_weight_kernel,
        out_shape=pltpu.VMEM((2, 3, 4 * width, 2 * mid), BF16),
        cost_estimate=pl.CostEstimate(flops=0, bytes_accessed=4 * 2**20, transcendentals=0),
        compiler_params=limited(4),
        name="token_weight",
    )(conv_in_weight)
    held = [pltpu.with_memory_space_constraint(value, pltpu.VMEM) for value in [token_weight, *mixed]]

    return pl.pallas_call(
        block_kernel,
        out_shape=jax.ShapeDtypeStruct((frames, 2, 2 * wide, mid), BF16),
        scratch_shapes=[
            pltpu.VMEM((2, 2, frames + 4, wide, 4 * width), BF16),
            pltpu.VMEM((4, 2, grown, wide, mid), BF16),
            pltpu.VMEM((2, 2, frames, wide, mid), BF16),
            pltpu.VMEM((16, grown, wide, mid), BF16),
            pltpu.VMEM((frames, 2, mid // LANES, 2 * wide, LANES), F32),
        ],
        compiler_params=limited(24),
        name="block",
    )(previous, own, held[0], conv_in_bias, norm_gain, *held[1:], conv_mid_bias)


def solution(mesh):
    return jax.shard_map(
        per_device,
        mesh=mesh,
        in_specs=(P("tm", None, "space", None), P(), P(), P(), P(), P()),
        out_specs=P("tm", "space", None, None),
        check_vma=False,
    )
```

```python
import functools

import jax
import jax.numpy as jnp
from jax import lax
from jax.experimental import pallas as pl
from jax.experimental.pallas import tpu as pltpu
from jax.sharding import PartitionSpec as P

BF16 = jnp.bfloat16
F32 = jnp.float32
LANES = 128


def dot(left, right):
    return jnp.dot(left, right, preferred_element_type=F32)


def moved_down(value):
    row = lax.broadcasted_iota(jnp.int32, value.shape, 0)
    return jnp.where(row == 0, 0.0, pltpu.roll(value, 1, 0))


def moved_up(value):
    rows = value.shape[0]
    row = lax.broadcasted_iota(jnp.int32, value.shape, 0)
    return jnp.where(row == rows - 1, 0.0, pltpu.roll(value, rows - 1, 0))


def position():
    return lax.axis_index("space")


def place(relative, tiles):
    bits = tiles.bit_length() - 1
    return sum((relative >> bit & 1) << (bits - 1 - bit) for bit in range(bits))


def chunks_kernel(own_ref, keep_ref, send_ref):
    frames, rows, _, _ = own_ref.shape
    half = rows // 2
    mine = position() // half
    for out_ref, part in ((keep_ref, mine), (send_ref, 1 - mine)):
        for at in range(half + 2):
            row = part * half + at - 1
            inside = jnp.logical_and(row >= 0, row < rows)
            value = own_ref[:, jnp.clip(row, 0, rows - 1)]
            value = jnp.where(inside, value, jnp.zeros_like(value))
            for pair in range(frames // 2):
                out_ref[0, at, pair] = jnp.concatenate([value[2 * pair], value[2 * pair + 1]], -1)


def halves_kernel(kept_ref, got_ref, keep_ref, send_ref):
    sources = kept_ref.shape[0]
    size = keep_ref.shape[1] - 2
    upper = position() // size % 2
    for at, ref in enumerate((kept_ref, got_ref)):
        to = slice(at * sources, (at + 1) * sources)
        keep_ref[to] = ref[:, pl.ds(upper * size, size + 2)]
        send_ref[to] = ref[:, pl.ds((1 - upper) * size, size + 2)]


def token_weight_kernel(conv_in_ref, token_weight_ref):
    ch = conv_in_ref.shape[3]
    mid = conv_in_ref.shape[4]
    token_weight_ref[...] = jnp.zeros_like(token_weight_ref)
    for time in range(3):
        for parity in range(2):
            for near in range(2):
                for b in range(3):
                    for e in range(3):
                        row = near + b
                        col = e + 1 - parity
                        at = (((col // 2) * 2 + row // 2) * 2 + row % 2) * 2 + col % 2
                        token_weight_ref[
                            parity, time, at * ch : (at + 1) * ch, near * mid : (near + 1) * mid
                        ] = conv_in_ref[time, b, e]


def mixed_kernel(time, conv_mid_ref, mixed_ref, taps, arrived):
    mid = conv_mid_ref.shape[-1]
    parts = arrived.shape[0]
    size = mid // parts
    step = 16

    def spread(g0, g1, g2):
        ends = g0 + g2
        return g0, ends + g1, ends - g1, g2

    def one(i, carry):
        at = pl.ds(pl.multiple_of(i * step, step), step)
        cols = [
            spread(*[taps[b, e, at, :].astype(F32) for b in range(3)]) for e in range(3)
        ]
        for u in range(4):
            for v, value in enumerate(spread(*[cols[e][u] for e in range(3)])):
                mixed_ref[u * 4 + v, at, :] = value.astype(BF16)
        return carry

    copies = []
    for part in range(parts):
        at = pl.ds(part * size, size)
        copies.append(
            pltpu.make_async_copy(
                conv_mid_ref.at[time, :, :, at], taps.at[:, :, at], arrived.at[part]
            )
        )
        copies[-1].start()
    for part in range(parts):
        copies[part].wait()
        lax.fori_loop(part * size // step, (part + 1) * size // step, one, 0)


def block_kernel(
    previous_ref,
    own_ref,
    token_weight_ref,
    in_bias_ref,
    gain_ref,
    mixed_0_ref,
    mixed_1_ref,
    mixed_2_ref,
    mid_bias_ref,
    out_ref,
    windows,
    active,
    feature,
    spectrum,
    lines,
):
    tiles, _, pairs, cols, pair = own_ref.shape
    wide = tiles * cols
    frames, rows, _, mid = out_ref.shape
    grown = frames + 2
    width = pair // 2
    me = position()

    with jax.named_scope("windows"):
        for part, ref in enumerate((previous_ref, own_ref)):
            got = [ref[place(tile ^ me, tiles)].astype(F32) for tile in range(tiles)]
            for two in range(pairs):
                line = [
                    jnp.concatenate([value[near, two] for value in got], 0) for near in range(3)
                ]
                for half in range(2):
                    above, below = line[half], line[half + 1]
                    for odd in range(2):
                        f = 2 * (part * pairs + two) + odd
                        at = slice(odd * width, (odd + 1) * width)
                        value = jnp.concatenate([above[:, at], below[:, at]], -1)
                        here = value.astype(BF16)
                        windows[0, half, f] = jnp.concatenate(
                            [moved_down(value).astype(BF16), here], -1
                        )
                        windows[1, half, f] = jnp.concatenate(
                            [here, moved_up(value).astype(BF16)], -1
                        )

    in_bias = in_bias_ref[...].reshape(1, mid)
    half_gain = gain_ref[...].reshape(1, mid) * 0.5
    first = (lax.axis_index("tm") > 0).astype(F32)
    top = (me > 0).astype(F32)
    bottom = (me < tiles - 1).astype(F32)
    with jax.named_scope("features"):
        for parity in range(2):
            weight = token_weight_ref[parity].reshape(6 * pair, 2 * mid)
            for half in range(2):
                left = jnp.concatenate(
                    [
                        windows[parity, half, a : a + grown].reshape(grown * wide, 2 * pair)
                        for a in range(3)
                    ],
                    -1,
                )
                summed = dot(left, weight)
                for near in range(2):
                    row = half * 2 + near
                    rounded = (summed[:, near * mid : (near + 1) * mid] + in_bias).astype(BF16)
                    if row in (1, 2):
                        feature[row - 1, parity] = rounded[2 * wide :].reshape(frames, wide, mid)
                    value = rounded.astype(F32)
                    mean = jnp.mean(value * value, axis=-1, keepdims=True)
                    scale = lax.rsqrt(mean + 1e-06)
                    if row == 0:
                        scale = scale * top
                    if row == 3:
                        scale = scale * bottom
                    scale = jnp.concatenate([scale[: 2 * wide] * first, scale[2 * wide :]], 0)
                    h = value * scale * half_gain
                    active[row, parity] = (h + h * jnp.tanh(h)).astype(BF16).reshape(grown, wide, mid)

    with jax.named_scope("spectrum"):

        def one_frame(f, carry):
            cells = []
            for row in range(4):
                even = active[row, 0, f].astype(F32)
                odd = active[row, 1, f].astype(F32)
                cells.append(
                    (moved_down(odd) - odd, even + odd, odd - even, even - moved_up(even))
                )
            for v in range(4):
                r0, r1, r2, r3 = [cells[row][v] for row in range(4)]
                spectrum[v, f] = (r0 - r2).astype(BF16)
                spectrum[4 + v, f] = (r1 + r2).astype(BF16)
                spectrum[8 + v, f] = (r2 - r1).astype(BF16)
                spectrum[12 + v, f] = (r1 - r3).astype(BF16)
            return carry

        lax.fori_loop(0, grown, one_frame, 0)

    def back(m0, m1, m2, m3):
        return m0 + 0.5 * (m1 + m2), 0.5 * (m1 - m2) - m3

    with jax.named_scope("mix"):
        mixed = (mixed_0_ref, mixed_1_ref, mixed_2_ref)
        sums = []
        for u in range(4):
            parts = []
            for v in range(4):
                at = u * 4 + v
                left = jnp.concatenate(
                    [
                        spectrum[at, a : a + frames].reshape(frames * wide, mid)
                        for a in range(3)
                    ],
                    -1,
                )
                right = jnp.concatenate([ref[at] for ref in mixed], 0)
                parts.append(dot(left, right))
            sums.append(back(*parts))
        mid_bias = mid_bias_ref[...].reshape(1, mid)
        for parity in range(2):
            for row, total in enumerate(back(*[sums[u][parity] for u in range(4)])):
                total = (total + mid_bias).reshape(frames, wide, mid)
                total = total + feature[row, parity].astype(F32)
                for f in range(frames):
                    for lane in range(mid // LANES):
                        lines[f, row, lane, pl.ds(parity, wide, stride=2), :] = total[
                            f, :, lane * LANES : (lane + 1) * LANES
                        ]
        for f in range(frames):
            for row in range(rows):
                for lane in range(mid // LANES):
                    out_ref[f, row, :, lane * LANES : (lane + 1) * LANES] = lines[
                        f, row, lane
                    ].astype(BF16)


def limited(mebibytes):
    return pltpu.CompilerParams(vmem_limit_bytes=mebibytes * 2**20)


def after(value, *others):
    return lax.optimization_barrier((value, *others))[0]


def exchanged(keep, send, axis, beside):
    count = lax.axis_size(axis)
    size = count // 2
    while True:
        got = lax.ppermute(send, axis, [(one, one ^ size) for one in range(count)])
        done = beside(send)
        if size == 1:
            return after(jnp.concatenate([keep, got], 0), *done)
        size //= 2
        half = jax.ShapeDtypeStruct((2 * keep.shape[0], size + 2, *keep.shape[2:]), keep.dtype)
        keep, send = pl.pallas_call(
            halves_kernel, out_shape=(half, half), compiler_params=limited(2), name="halves"
        )(keep, got)
        send = after(send, *done)


def shifted(value, axis):
    count = lax.axis_size(axis)
    return lax.ppermute(value, axis, [(at, at + 1) for at in range(count - 1)])


def per_device(
    latent_tokens, conv_in_weight, conv_in_bias, norm_gain, conv_mid_weight, conv_mid_bias
):
    frames, token_rows, cols, width = latent_tokens.shape
    tiles = lax.axis_size("space")
    assert token_rows == tiles and tiles & (tiles - 1) == 0 and frames == 4
    mid = conv_mid_weight.shape[-1]
    wide = tiles * cols
    grown = frames + 2
    line = (frames // 2, cols, 2 * width)

    half = jax.ShapeDtypeStruct((1, tiles // 2 + 2) + line, BF16)
    keep, send = pl.pallas_call(chunks_kernel, out_shape=(half, half), compiler_params=limited(2), name="chunks")(
        latent_tokens
    )
    mixed = []

    def beside(value):
        time = len(mixed)
        if time == 3:
            return ()
        mixed.append(
            pl.pallas_call(
                functools.partial(mixed_kernel, time),
                out_shape=pltpu.VMEM((16, mid, mid), BF16),
                in_specs=[pl.BlockSpec(memory_space=pltpu.HBM)],
                scratch_shapes=[
                    pltpu.VMEM((3, 3, mid, mid), BF16),
                    pltpu.SemaphoreType.DMA((4,)),
                ],
                cost_estimate=pl.CostEstimate(
                    flops=0, bytes_accessed=50 * mid * mid, transcendentals=0
                ),
                compiler_params=limited(6),
                name="mixed",
            )(pltpu.with_memory_space_constraint(after(conv_mid_weight, value), pltpu.HBM))
        )
        return mixed[-1:]

    own = exchanged(keep, send, "space", beside)
    while len(mixed) < 3:
        beside(own)
    previous = shifted(own, "tm")
    token_weight = pl.pallas_call(
        token_weight_kernel,
        out_shape=pltpu.VMEM((2, 3, 4 * width, 2 * mid), BF16),
        cost_estimate=pl.CostEstimate(flops=0, bytes_accessed=4 * 2**20, transcendentals=0),
        compiler_params=limited(4),
        name="token_weight",
    )(conv_in_weight)
    held = [pltpu.with_memory_space_constraint(value, pltpu.VMEM) for value in [token_weight, *mixed]]

    return pl.pallas_call(
        block_kernel,
        out_shape=jax.ShapeDtypeStruct((frames, 2, 2 * wide, mid), BF16),
        scratch_shapes=[
            pltpu.VMEM((2, 2, frames + 4, wide, 4 * width), BF16),
            pltpu.VMEM((4, 2, grown, wide, mid), BF16),
            pltpu.VMEM((2, 2, frames, wide, mid), BF16),
            pltpu.VMEM((16, grown, wide, mid), BF16),
            pltpu.VMEM((frames, 2, mid // LANES, 2 * wide, LANES), F32),
        ],
        compiler_params=limited(24),
        name="block",
    )(previous, own, held[0], conv_in_bias, norm_gain, *held[1:], conv_mid_bias)


def solution(mesh):
    return jax.shard_map(
        per_device,
        mesh=mesh,
        in_specs=(P("tm", None, "space", None), P(), P(), P(), P(), P()),
        out_specs=P("tm", "space", None, None),
        check_vma=False,
    )
```

```python
import functools

import jax
import jax.numpy as jnp
from jax import lax
from jax.experimental import pallas as pl
from jax.experimental.pallas import tpu as pltpu
from jax.sharding import PartitionSpec as P

BF16 = jnp.bfloat16
F32 = jnp.float32
LANES = 128


def dot(left, right):
    return jnp.dot(left, right, preferred_element_type=F32)


def moved_down(value):
    row = lax.broadcasted_iota(jnp.int32, value.shape, 0)
    return jnp.where(row == 0, 0.0, pltpu.roll(value, 1, 0))


def moved_up(value):
    rows = value.shape[0]
    row = lax.broadcasted_iota(jnp.int32, value.shape, 0)
    return jnp.where(row == rows - 1, 0.0, pltpu.roll(value, rows - 1, 0))


def position():
    return lax.axis_index("space")


def place(relative, tiles):
    bits = tiles.bit_length() - 1
    return sum((relative >> bit & 1) << (bits - 1 - bit) for bit in range(bits))


def chunks_kernel(own_ref, keep_ref, send_ref):
    frames, rows, _, _ = own_ref.shape
    half = rows // 2
    mine = position() // half
    for out_ref, part in ((keep_ref, mine), (send_ref, 1 - mine)):
        for at in range(half + 2):
            row = part * half + at - 1
            inside = jnp.logical_and(row >= 0, row < rows)
            value = own_ref[:, jnp.clip(row, 0, rows - 1)]
            value = jnp.where(inside, value, jnp.zeros_like(value))
            for pair in range(frames // 2):
                out_ref[0, at, pair] = jnp.concatenate([value[2 * pair], value[2 * pair + 1]], -1)


def halves_kernel(kept_ref, got_ref, keep_ref, send_ref):
    sources = kept_ref.shape[0]
    size = keep_ref.shape[1] - 2
    upper = position() // size % 2
    for at, ref in enumerate((kept_ref, got_ref)):
        to = slice(at * sources, (at + 1) * sources)
        keep_ref[to] = ref[:, pl.ds(upper * size, size + 2)]
        send_ref[to] = ref[:, pl.ds((1 - upper) * size, size + 2)]


def token_weight_kernel(conv_in_ref, token_weight_ref):
    ch = conv_in_ref.shape[3]
    mid = conv_in_ref.shape[4]
    for time in range(3):
        for parity in range(2):
            for near in range(2):
                to = slice(near * mid, (near + 1) * mid)
                for row in range(4):
                    for col in range(4):
                        b = row - near
                        e = col - 1 + parity
                        at = (((col // 2) * 2 + row // 2) * 2 + row % 2) * 2 + col % 2
                        inside = 0 <= b < 3 and 0 <= e < 3
                        token_weight_ref[parity, time, at * ch : (at + 1) * ch, to] = (
                            conv_in_ref[time, b, e] if inside else jnp.zeros((ch, mid), BF16)
                        )


def mixed_kernel(time, conv_mid_ref, mixed_ref, taps, arrived):
    mid = conv_mid_ref.shape[-1]
    parts = arrived.shape[0]
    size = mid // parts
    step = 16

    def spread(g0, g1, g2):
        ends = g0 + g2
        return g0, ends + g1, ends - g1, g2

    def one(i, carry):
        at = pl.ds(pl.multiple_of(i * step, step), step)
        cols = [
            spread(*[taps[b, e, at, :].astype(F32) for b in range(3)]) for e in range(3)
        ]
        for u in range(4):
            for v, value in enumerate(spread(*[cols[e][u] for e in range(3)])):
                mixed_ref[u * 4 + v, at, :] = value.astype(BF16)
        return carry

    copies = []
    for part in range(parts):
        at = pl.ds(part * size, size)
        copies.append(
            pltpu.make_async_copy(
                conv_mid_ref.at[time, :, :, at], taps.at[:, :, at], arrived.at[part]
            )
        )
        copies[-1].start()
    for part in range(parts):
        copies[part].wait()
        lax.fori_loop(part * size // step, (part + 1) * size // step, one, 0)


def windows(ref, first, out):
    tiles, _, pairs, cols, pair = ref.shape
    width = pair // 2
    me = position()
    got = [ref[place(tile ^ me, tiles)].astype(F32) for tile in range(tiles)]
    for two in range(pairs):
        line = [jnp.concatenate([value[near, two] for value in got], 0) for near in range(3)]
        for half in range(2):
            above, below = line[half], line[half + 1]
            for odd in range(2):
                f = first + 2 * two + odd
                at = slice(odd * width, (odd + 1) * width)
                value = jnp.concatenate([above[:, at], below[:, at]], -1)
                here = value.astype(BF16)
                out[0, half, f] = jnp.concatenate([moved_down(value).astype(BF16), here], -1)
                out[1, half, f] = jnp.concatenate([here, moved_up(value).astype(BF16)], -1)


def stacked(take, frames):
    return jnp.concatenate(
        [jnp.concatenate([take(f + a) for f in frames], 0) for a in range(3)], -1
    )


def activate(take, frames, blank, tiles, weight_ref, in_bias_ref, gain_ref, active, feature, evens=lambda: None):
    mid = gain_ref.shape[0]
    in_bias = in_bias_ref[...].reshape(1, mid)
    half_gain = gain_ref[...].reshape(1, mid) * 0.5
    me = position()
    started = (lax.axis_index("tm") > 0).astype(F32)
    top = (me > 0).astype(F32)
    bottom = (me < tiles - 1).astype(F32)
    for parity in range(2):
        if parity == 1:
            evens()
        weight = weight_ref[parity].reshape(-1, 2 * mid)
        for half in range(2):
            left = stacked(lambda f: take(parity, half, f), frames)
            wide = left.shape[0] // len(frames)
            summed = dot(left, weight)
            for near in range(2):
                row = half * 2 + near
                rounded = (summed[:, near * mid : (near + 1) * mid] + in_bias).astype(BF16)
                if row in (1, 2):
                    feature[row - 1, parity] = rounded[blank * wide :].reshape(-1, wide, mid)
                value = rounded.astype(F32)
                mean = jnp.mean(value * value, axis=-1, keepdims=True)
                scale = lax.rsqrt(mean + 1e-06)
                if row == 0:
                    scale = scale * top
                if row == 3:
                    scale = scale * bottom
                if blank:
                    scale = jnp.concatenate(
                        [scale[: blank * wide] * started, scale[blank * wide :]], 0
                    )
                h = value * scale * half_gain
                active[row, parity] = (
                    (h + h * jnp.tanh(h)).astype(BF16).reshape(len(frames), wide, mid)
                )


def transform(active, f, u, spectrum, parts=range(4)):
    def over_rows(parity):
        r = [active[row, parity, f].astype(F32) for row in ((0, 2), (1, 2), (2, 1), (1, 3))[u]]
        return r[0] + r[1] if u == 1 else r[0] - r[1]

    even = over_rows(0) if set(parts) - {0} else None
    odd = over_rows(1) if set(parts) - {3} else None
    for v in parts:
        if v == 0:
            value = moved_down(odd) - odd
        elif v == 1:
            value = even + odd
        elif v == 2:
            value = odd - even
        else:
            value = even - moved_up(even)
        spectrum[u * 4 + v, f] = value.astype(BF16)


def front_kernel(
    own_ref, token_weight_ref, in_bias_ref, gain_ref, windows_ref, feature_ref, spectrum_ref, active
):
    windows(own_ref, 0, windows_ref)
    activate(
        lambda parity, half, f: windows_ref[parity, half, f],
        range(windows_ref.shape[2] - 2),
        0,
        own_ref.shape[0],
        token_weight_ref,
        in_bias_ref,
        gain_ref,
        active,
        feature_ref,
    )
    for u in range(4):
        for f in range(active.shape[2]):
            transform(active, f, u, spectrum_ref)


def block_kernel(
    previous_ref,
    windows_ref,
    late_feature_ref,
    late_spectrum_ref,
    token_weight_ref,
    in_bias_ref,
    gain_ref,
    mixed_0_ref,
    mixed_1_ref,
    mixed_2_ref,
    mid_bias_ref,
    out_ref,
    early_windows,
    active,
    feature,
    spectrum,
    lines,
    rounded,
    sent,
):
    tiles = previous_ref.shape[0]
    frames, rows, _, mid = out_ref.shape
    held = early_windows.shape[2]
    early = spectrum.shape[1]
    late = frames - late_feature_ref.shape[2]
    wide = spectrum.shape[2]

    windows(previous_ref, 0, early_windows)
    activate(
        lambda parity, half, f: (
            early_windows[parity, half, f]
            if f < held
            else windows_ref[parity, half, f - held]
        ),
        range(early),
        2,
        tiles,
        token_weight_ref,
        in_bias_ref,
        gain_ref,
        active,
        feature,
        lambda: [transform(active, f, u, spectrum, (3,)) for u in range(4) for f in range(early)],
    )

    def back(m0, m1, m2, m3):
        return m0 + 0.5 * (m1 + m2), 0.5 * (m1 - m2) - m3

    def product(at):
        def take(f):
            return spectrum[at, f] if f < early else late_spectrum_ref[at, f - early]

        right = jnp.concatenate([ref[at] for ref in (mixed_0_ref, mixed_1_ref, mixed_2_ref)], 0)
        return dot(stacked(take, range(frames)), right)

    mid_bias = mid_bias_ref[...].reshape(1, mid)

    def finish(row, totals):
        for parity in range(2):
            total = (totals[parity] + mid_bias).reshape(frames, wide, mid)
            for f in range(frames):
                held_feature = (
                    feature[row, parity, f] if f < late else late_feature_ref[row, parity, f - late]
                )
                value = total[f] + held_feature.astype(F32)
                for lane in range(mid // LANES):
                    lines[f, lane, pl.ds(parity, wide, stride=2), :] = value[
                        :, lane * LANES : (lane + 1) * LANES
                    ]
        for f in range(frames):
            for lane in range(mid // LANES):
                rounded[row, f, :, lane * LANES : (lane + 1) * LANES] = lines[f, lane].astype(BF16)
        copy = pltpu.make_async_copy(rounded.at[row], out_ref.at[:, row], sent.at[row])
        copy.start()
        return copy

    def chores(u):
        return [functools.partial(transform, active, f, u, spectrum, (0, 1, 2)) for f in range(early)]

    last = []
    todo = chores(0) + chores(1)
    for u in range(4):
        last.append(product(u * 4 + 3))
        for chore in todo[2 * u : 2 * u + 2]:
            chore()
    sums = []
    copies = []
    for u in range(4):
        todo = chores(u + 2) if u < 2 else []
        parts = []
        for v in range(3):
            parts.append(product(u * 4 + v))
            for chore in todo[v::3]:
                chore()
        sums.append(back(*parts, last[u]))
        if u == 2:
            totals = [sums[0][p] + 0.5 * (sums[1][p] + sums[2][p]) for p in range(2)]
            copies.append(finish(0, totals))
    totals = [0.5 * (sums[1][p] - sums[2][p]) - sums[3][p] for p in range(2)]
    copies.append(finish(1, totals))
    for copy in copies:
        copy.wait()


def limited(mebibytes):
    return pltpu.CompilerParams(vmem_limit_bytes=mebibytes * 2**20)


def after(value, *others):
    return lax.optimization_barrier((value, *others))[0]


def fast(value):
    return pltpu.with_memory_space_constraint(value, pltpu.VMEM)


def far(value):
    return pltpu.with_memory_space_constraint(value, pltpu.HBM)


def exchanged(keep, send, axis, beside):
    count = lax.axis_size(axis)
    size = count // 2
    while True:
        got = lax.ppermute(send, axis, [(one, one ^ size) for one in range(count)])
        done = beside(send)
        if size == 1:
            return after(jnp.concatenate([keep, got], 0), *done)
        size //= 2
        half = jax.ShapeDtypeStruct((2 * keep.shape[0], size + 2, *keep.shape[2:]), keep.dtype)
        keep, send = pl.pallas_call(
            halves_kernel, out_shape=(half, half), compiler_params=limited(2), name="halves"
        )(keep, got)
        send = after(send, *done)


def shifted(value, axis):
    count = lax.axis_size(axis)
    return lax.ppermute(value, axis, [(at, at + 1) for at in range(count - 1)])


def per_device(
    latent_tokens, conv_in_weight, conv_in_bias, norm_gain, conv_mid_weight, conv_mid_bias
):
    frames, token_rows, cols, width = latent_tokens.shape
    tiles = lax.axis_size("space")
    assert token_rows == tiles and tiles & (tiles - 1) == 0 and frames == 4
    mid = conv_mid_weight.shape[-1]
    wide = tiles * cols
    line = (frames // 2, cols, 2 * width)

    half = jax.ShapeDtypeStruct((1, tiles // 2 + 2) + line, BF16)
    keep, send = pl.pallas_call(chunks_kernel, out_shape=(half, half), compiler_params=limited(2), name="chunks")(
        latent_tokens
    )
    mixed = []

    def beside(value):
        time = len(mixed)
        if time == 3:
            return ()
        weight = far(after(conv_mid_weight, value))
        mixed.append(
            pl.pallas_call(
                functools.partial(mixed_kernel, time),
                out_shape=pltpu.VMEM((16, mid, mid), BF16),
                in_specs=[pl.BlockSpec(memory_space=pltpu.HBM)],
                scratch_shapes=[pltpu.VMEM((3, 3, mid, mid), BF16), pltpu.SemaphoreType.DMA((4,))],
                cost_estimate=pl.CostEstimate(
                    flops=0, bytes_accessed=50 * mid * mid, transcendentals=0
                ),
                compiler_params=limited(6),
                name="mixed",
            )(weight)
        )
        if time < 2:
            return mixed[-1:]
        token_weight.append(
            pl.pallas_call(
                token_weight_kernel,
                out_shape=pltpu.VMEM((2, 3, 4 * width, 2 * mid), BF16),
                cost_estimate=pl.CostEstimate(
                    flops=0, bytes_accessed=4 * 2**20, transcendentals=0
                ),
                compiler_params=limited(4),
                name="token_weight",
            )(conv_in_weight)
        )
        return mixed[-1:] + token_weight

    token_weight = []
    own = exchanged(keep, send, "space", beside)
    while len(mixed) < 3:
        beside(own)
    previous = shifted(own, "tm")

    late = 2
    early = frames + 2 - late
    windows_shape = (2, 2, frames, wide, 4 * width)
    own_windows, late_feature, late_spectrum = pl.pallas_call(
        front_kernel,
        out_shape=(
            pltpu.VMEM(windows_shape, BF16),
            pltpu.VMEM((2, 2, late, wide, mid), BF16),
            pltpu.VMEM((16, late, wide, mid), BF16),
        ),
        scratch_shapes=[pltpu.VMEM((4, 2, late, wide, mid), BF16)],
        cost_estimate=pl.CostEstimate(
            flops=0, bytes_accessed=50 * mid * mid, transcendentals=0
        ),
        compiler_params=limited(8),
        name="front",
    )(own, fast(token_weight[0]), conv_in_bias, norm_gain)

    return pl.pallas_call(
        block_kernel,
        out_shape=jax.ShapeDtypeStruct((frames, 2, 2 * wide, mid), BF16),
        out_specs=pl.BlockSpec(memory_space=pltpu.HBM),
        scratch_shapes=[
            pltpu.VMEM(windows_shape, BF16),
            pltpu.VMEM((4, 2, early, wide, mid), BF16),
            pltpu.VMEM((2, 2, frames - late, wide, mid), BF16),
            pltpu.VMEM((16, early, wide, mid), BF16),
            pltpu.VMEM((frames, mid // LANES, 2 * wide, LANES), F32),
            pltpu.VMEM((2, frames, 2 * wide, mid), BF16),
            pltpu.SemaphoreType.DMA((2,)),
        ],
        compiler_params=limited(24),
        name="block",
    )(
        previous,
        fast(own_windows),
        fast(late_feature),
        fast(late_spectrum),
        fast(token_weight[0]),
        conv_in_bias,
        norm_gain,
        *[fast(value) for value in mixed],
        conv_mid_bias,
    )


def solution(mesh):
    return jax.shard_map(
        per_device,
        mesh=mesh,
        in_specs=(P("tm", None, "space", None), P(), P(), P(), P(), P()),
        out_specs=P("tm", "space", None, None),
        check_vma=False,
    )
```

```python
import functools

import jax
import jax.numpy as jnp
from jax import lax
from jax.experimental import pallas as pl
from jax.experimental.pallas import tpu as pltpu
from jax.sharding import PartitionSpec as P

BF16 = jnp.bfloat16
F32 = jnp.float32
LANES = 128
SUBLANES = 8


def dot(left, right):
    return jnp.dot(left, right, preferred_element_type=F32)


def moved_down(value):
    value = pltpu.roll(value, 1, 0)
    head = value[:SUBLANES]
    row = lax.broadcasted_iota(jnp.int32, head.shape, 0)
    return jnp.concatenate([jnp.where(row == 0, 0.0, head), value[SUBLANES:]], 0)


def moved_up(value):
    rows = value.shape[0]
    value = pltpu.roll(value, rows - 1, 0)
    tail = value[rows - SUBLANES :]
    row = lax.broadcasted_iota(jnp.int32, tail.shape, 0)
    return jnp.concatenate(
        [value[: rows - SUBLANES], jnp.where(row == SUBLANES - 1, 0.0, tail)], 0
    )


def position():
    return lax.axis_index("space")


def place(relative, tiles):
    bits = tiles.bit_length() - 1
    return sum((relative >> bit & 1) << (bits - 1 - bit) for bit in range(bits))


def chunks_kernel(own_ref, keep_ref, send_ref):
    frames, rows, _, _ = own_ref.shape
    half = rows // 2
    mine = position() // half
    for out_ref, part in ((keep_ref, mine), (send_ref, 1 - mine)):
        for at in range(half + 2):
            row = part * half + at - 1
            inside = jnp.logical_and(row >= 0, row < rows)
            value = own_ref[:, jnp.clip(row, 0, rows - 1)]
            value = jnp.where(inside, value, jnp.zeros_like(value))
            for pair in range(frames // 2):
                out_ref[0, at, pair] = jnp.concatenate([value[2 * pair], value[2 * pair + 1]], -1)


def halves_kernel(kept_ref, got_ref, keep_ref, send_ref):
    sources = kept_ref.shape[0]
    size = keep_ref.shape[1] - 2
    upper = position() // size % 2
    for at, ref in enumerate((kept_ref, got_ref)):
        to = slice(at * sources, (at + 1) * sources)
        keep_ref[to] = ref[:, pl.ds(upper * size, size + 2)]
        send_ref[to] = ref[:, pl.ds((1 - upper) * size, size + 2)]


def token_weight_kernel(conv_in_ref, token_weight_ref):
    ch = conv_in_ref.shape[3]
    mid = conv_in_ref.shape[4]
    for time in range(3):
        for parity in range(2):
            for near in range(2):
                to = slice(near * mid, (near + 1) * mid)
                for row in range(4):
                    for col in range(4):
                        b = row - near
                        e = col - 1 + parity
                        at = (((col // 2) * 2 + row // 2) * 2 + row % 2) * 2 + col % 2
                        inside = 0 <= b < 3 and 0 <= e < 3
                        token_weight_ref[parity, time, at * ch : (at + 1) * ch, to] = (
                            conv_in_ref[time, b, e] if inside else jnp.zeros((ch, mid), BF16)
                        )


def mixed_kernel(time, conv_mid_ref, mixed_ref, taps, arrived):
    mid = conv_mid_ref.shape[-1]
    parts = arrived.shape[0]
    size = mid // parts
    step = 16

    def spread(g0, g1, g2):
        ends = g0 + g2
        return g0, ends + g1, ends - g1, g2

    def one(i, carry):
        at = pl.ds(pl.multiple_of(i * step, step), step)
        cols = [
            spread(*[taps[b, e, at, :].astype(F32) for b in range(3)]) for e in range(3)
        ]
        for u in range(4):
            for v, value in enumerate(spread(*[cols[e][u] for e in range(3)])):
                mixed_ref[u * 4 + v, at, :] = value.astype(BF16)
        return carry

    copies = []
    for part in range(parts):
        at = pl.ds(part * size, size)
        copies.append(
            pltpu.make_async_copy(
                conv_mid_ref.at[time, :, :, at], taps.at[:, :, at], arrived.at[part]
            )
        )
        copies[-1].start()
    for part in range(parts):
        copies[part].wait()
        lax.fori_loop(part * size // step, (part + 1) * size // step, one, 0)


def windows(ref, first, out, valid=None):
    tiles, _, pairs, cols, pair = ref.shape
    width = pair // 2
    me = position()
    got = [ref[place(tile ^ me, tiles)].astype(F32) for tile in range(tiles)]
    for two in range(pairs):
        line = [jnp.concatenate([value[near, two] for value in got], 0) for near in range(3)]
        if valid is not None:
            line = [jnp.where(valid, value, 0.0) for value in line]
        for half in range(2):
            above, below = line[half], line[half + 1]
            for odd in range(2):
                f = first + 2 * two + odd
                at = slice(odd * width, (odd + 1) * width)
                value = jnp.concatenate([above[:, at], below[:, at]], -1)
                here = value.astype(BF16)
                out[0, half, f] = jnp.concatenate([moved_down(value).astype(BF16), here], -1)
                out[1, half, f] = jnp.concatenate([here, moved_up(value).astype(BF16)], -1)


def stacked(take, frames):
    return jnp.concatenate(
        [jnp.concatenate([take(f + a) for f in frames], 0) for a in range(3)], -1
    )


def activate(take, frames, blank, tiles, weight_ref, in_bias_ref, gain_ref, active, feature, evens=lambda: None):
    mid = gain_ref.shape[0]
    in_bias = in_bias_ref[...].reshape(1, mid)
    half_gain = gain_ref[...].reshape(1, mid) * 0.5
    me = position()
    started = (lax.axis_index("tm") > 0).astype(F32)
    top = (me > 0).astype(F32)
    bottom = (me < tiles - 1).astype(F32)
    for parity in range(2):
        if parity == 1:
            evens()
        weight = weight_ref[parity].reshape(-1, 2 * mid)
        for half in range(2):
            left = stacked(lambda f: take(parity, half, f), frames)
            wide = left.shape[0] // len(frames)
            summed = dot(left, weight)
            for near in range(2):
                row = half * 2 + near
                rounded = (summed[:, near * mid : (near + 1) * mid] + in_bias).astype(BF16)
                if row in (1, 2):
                    feature[row - 1, parity] = rounded[blank * wide :].reshape(-1, wide, mid)
                value = rounded.astype(F32)
                mean = jnp.mean(value * value, axis=-1, keepdims=True)
                scale = lax.rsqrt(mean + 1e-06)
                if row == 0:
                    scale = scale * top
                if row == 3:
                    scale = scale * bottom
                if blank:
                    scale = jnp.concatenate(
                        [scale[: blank * wide] * started, scale[blank * wide :]], 0
                    )
                h = value * scale * half_gain
                active[row, parity] = (
                    (h + h * jnp.tanh(h)).astype(BF16).reshape(len(frames), wide, mid)
                )


def transform(active, f, u, spectrum, parts=range(4)):
    def over_rows(parity):
        r = [active[row, parity, f].astype(F32) for row in ((0, 2), (1, 2), (2, 1), (1, 3))[u]]
        return r[0] + r[1] if u == 1 else r[0] - r[1]

    even = over_rows(0) if set(parts) - {0} else None
    odd = over_rows(1) if set(parts) - {3} else None
    for v in parts:
        if v == 0:
            value = moved_down(odd) - odd
        elif v == 1:
            value = even + odd
        elif v == 2:
            value = odd - even
        else:
            value = even - moved_up(even)
        spectrum[u * 4 + v][f] = value.astype(BF16)


def front_kernel(
    own_ref, token_weight_ref, in_bias_ref, gain_ref, windows_ref, feature_ref, spectrum_ref, active
):
    windows(own_ref, 0, windows_ref)
    activate(
        lambda parity, half, f: windows_ref[parity, half, f],
        range(windows_ref.shape[2] - 2),
        0,
        own_ref.shape[0],
        token_weight_ref,
        in_bias_ref,
        gain_ref,
        active,
        feature_ref,
    )
    parts = [spectrum_ref.at[at] for at in range(16)]
    for u in range(4):
        for f in range(active.shape[2]):
            transform(active, f, u, parts)


def block_kernel(
    previous_ref,
    windows_ref,
    late_feature_ref,
    late_spectrum_ref,
    token_weight_ref,
    in_bias_ref,
    gain_ref,
    mixed_0_ref,
    mixed_1_ref,
    mixed_2_ref,
    mid_bias_ref,
    out_ref,
    early_windows,
    active,
    feature,
    spectrum,
    lines,
    rounded,
    sent,
):
    tiles = previous_ref.shape[0]
    frames, rows, _, mid = out_ref.shape
    held = early_windows.shape[2]
    early = spectrum[0].shape[0]
    late = frames - late_feature_ref.shape[2]
    wide = spectrum[0].shape[1]

    windows(previous_ref, 0, early_windows, lax.axis_index("tm") > 0)
    activate(
        lambda parity, half, f: (
            early_windows[parity, half, f]
            if f < held
            else windows_ref[parity, half, f - held]
        ),
        range(early),
        2,
        tiles,
        token_weight_ref,
        in_bias_ref,
        gain_ref,
        active,
        feature,
        lambda: [transform(active, f, u, spectrum, (3,)) for u in range(4) for f in range(early)],
    )

    def back(m0, m1, m2, m3):
        return m0 + 0.5 * (m1 + m2), 0.5 * (m1 - m2) - m3

    def product(at):
        def take(f):
            return spectrum[at][f] if f < early else late_spectrum_ref[at, f - early]

        right = jnp.concatenate([ref[at] for ref in (mixed_0_ref, mixed_1_ref, mixed_2_ref)], 0)
        return dot(stacked(take, range(frames)), right)

    mid_bias = mid_bias_ref[...].reshape(1, mid)

    def finish(row, totals):
        for parity in range(2):
            total = (totals[parity] + mid_bias).reshape(frames, wide, mid)
            for f in range(frames):
                held_feature = (
                    feature[row, parity, f] if f < late else late_feature_ref[row, parity, f - late]
                )
                value = total[f] + held_feature.astype(F32)
                for lane in range(mid // LANES):
                    lines[f, lane, pl.ds(parity, wide, stride=2), :] = value[
                        :, lane * LANES : (lane + 1) * LANES
                    ]
        for f in range(frames):
            for lane in range(mid // LANES):
                rounded[row, f, :, lane * LANES : (lane + 1) * LANES] = lines[f, lane].astype(BF16)
        copy = pltpu.make_async_copy(rounded.at[row], out_ref.at[:, row], sent.at[row])
        copy.start()
        return copy

    def chores(u):
        return [functools.partial(transform, active, f, u, spectrum, (0, 1, 2)) for f in range(early)]

    last = []
    todo = chores(0) + chores(1)
    for u in range(4):
        last.append(product(u * 4 + 3))
        for chore in todo[2 * u : 2 * u + 2]:
            chore()
    sums = []
    copies = []
    for u in range(4):
        todo = chores(u + 2) if u < 2 else []
        parts = []
        for v in range(3):
            parts.append(product(u * 4 + v))
            for chore in todo[v::3]:
                chore()
        sums.append(back(*parts, last[u]))
        if u == 2:
            totals = [sums[0][p] + 0.5 * (sums[1][p] + sums[2][p]) for p in range(2)]
            copies.append(finish(0, totals))
    totals = [0.5 * (sums[1][p] - sums[2][p]) - sums[3][p] for p in range(2)]
    copies.append(finish(1, totals))
    for copy in copies:
        copy.wait()


def limited(mebibytes):
    return pltpu.CompilerParams(vmem_limit_bytes=mebibytes * 2**20)


def after(value, *others):
    return lax.optimization_barrier((value, *others))[0]


def fast(value):
    return pltpu.with_memory_space_constraint(value, pltpu.VMEM)


def far(value):
    return pltpu.with_memory_space_constraint(value, pltpu.HBM)


def exchanged(keep, send, axis, beside):
    count = lax.axis_size(axis)
    size = count // 2
    while True:
        got = lax.ppermute(send, axis, [(one, one ^ size) for one in range(count)])
        done = beside(send)
        if size == 1:
            return after(jnp.concatenate([keep, got], 0), *done)
        size //= 2
        half = jax.ShapeDtypeStruct((2 * keep.shape[0], size + 2, *keep.shape[2:]), keep.dtype)
        keep, send = pl.pallas_call(
            halves_kernel, out_shape=(half, half), compiler_params=limited(2), name="halves"
        )(keep, got)
        send = after(send, *done)


def shifted(value, axis):
    count = lax.axis_size(axis)
    return lax.ppermute(value, axis, [(at, (at + 1) % count) for at in range(count)])


def per_device(
    latent_tokens, conv_in_weight, conv_in_bias, norm_gain, conv_mid_weight, conv_mid_bias
):
    frames, token_rows, cols, width = latent_tokens.shape
    tiles = lax.axis_size("space")
    assert token_rows == tiles and tiles & (tiles - 1) == 0 and frames == 4
    mid = conv_mid_weight.shape[-1]
    wide = tiles * cols
    line = (frames // 2, cols, 2 * width)

    half = jax.ShapeDtypeStruct((1, tiles // 2 + 2) + line, BF16)
    keep, send = pl.pallas_call(chunks_kernel, out_shape=(half, half), compiler_params=limited(2), name="chunks")(
        latent_tokens
    )
    mixed = []

    def beside(value):
        time = len(mixed)
        if time == 3:
            return ()
        weight = far(after(conv_mid_weight, value))
        mixed.append(
            pl.pallas_call(
                functools.partial(mixed_kernel, time),
                out_shape=pltpu.VMEM((16, mid, mid), BF16),
                in_specs=[pl.BlockSpec(memory_space=pltpu.HBM)],
                scratch_shapes=[pltpu.VMEM((3, 3, mid, mid), BF16), pltpu.SemaphoreType.DMA((4,))],
                cost_estimate=pl.CostEstimate(
                    flops=0, bytes_accessed=50 * mid * mid, transcendentals=0
                ),
                compiler_params=limited(6),
                name="mixed",
            )(weight)
        )
        if time < 2:
            return mixed[-1:]
        token_weight.append(
            pl.pallas_call(
                token_weight_kernel,
                out_shape=pltpu.VMEM((2, 3, 4 * width, 2 * mid), BF16),
                cost_estimate=pl.CostEstimate(
                    flops=0, bytes_accessed=4 * 2**20, transcendentals=0
                ),
                compiler_params=limited(4),
                name="token_weight",
            )(conv_in_weight)
        )
        return mixed[-1:] + token_weight

    token_weight = []
    own = exchanged(keep, send, "space", beside)
    while len(mixed) < 3:
        beside(own)
    previous = shifted(own, "tm")

    late = 2
    early = frames + 2 - late
    windows_shape = (2, 2, frames, wide, 4 * width)
    own_windows, late_feature, late_spectrum = pl.pallas_call(
        front_kernel,
        out_shape=(
            pltpu.VMEM(windows_shape, BF16),
            pltpu.VMEM((2, 2, late, wide, mid), BF16),
            pltpu.VMEM((16, late, wide, mid), BF16),
        ),
        scratch_shapes=[pltpu.VMEM((4, 2, late, wide, mid), BF16)],
        cost_estimate=pl.CostEstimate(
            flops=0, bytes_accessed=50 * mid * mid, transcendentals=0
        ),
        compiler_params=limited(8),
        name="front",
    )(own, fast(token_weight[0]), conv_in_bias, norm_gain)

    return pl.pallas_call(
        block_kernel,
        out_shape=jax.ShapeDtypeStruct((frames, 2, 2 * wide, mid), BF16),
        out_specs=pl.BlockSpec(memory_space=pltpu.HBM),
        scratch_shapes=[
            pltpu.VMEM(windows_shape, BF16),
            pltpu.VMEM((4, 2, early, wide, mid), BF16),
            pltpu.VMEM((2, 2, frames - late, wide, mid), BF16),
            [pltpu.VMEM((early, wide, mid), BF16) for _ in range(16)],
            pltpu.VMEM((frames, mid // LANES, 2 * wide, LANES), F32),
            pltpu.VMEM((2, frames, 2 * wide, mid), BF16),
            pltpu.SemaphoreType.DMA((2,)),
        ],
        compiler_params=limited(24),
        name="block",
    )(
        previous,
        fast(own_windows),
        fast(late_feature),
        fast(late_spectrum),
        fast(token_weight[0]),
        conv_in_bias,
        norm_gain,
        *[fast(value) for value in mixed],
        conv_mid_bias,
    )


def solution(mesh):
    return jax.shard_map(
        per_device,
        mesh=mesh,
        in_specs=(P("tm", None, "space", None), P(), P(), P(), P(), P()),
        out_specs=P("tm", "space", None, None),
        check_vma=False,
    )
```

```python
import functools

import jax
import jax.numpy as jnp
from jax import lax
from jax.experimental import pallas as pl
from jax.experimental.pallas import tpu as pltpu
from jax.sharding import PartitionSpec as P

BF16 = jnp.bfloat16
F32 = jnp.float32
LANES = 128
SUBLANES = 8


def dot(left, right):
    return jnp.dot(left, right, preferred_element_type=F32)


def moved_down(value):
    value = pltpu.roll(value, 1, 0)
    head = value[:SUBLANES]
    row = lax.broadcasted_iota(jnp.int32, head.shape, 0)
    return jnp.concatenate([jnp.where(row == 0, 0.0, head), value[SUBLANES:]], 0)


def moved_up(value):
    rows = value.shape[0]
    value = pltpu.roll(value, rows - 1, 0)
    tail = value[rows - SUBLANES :]
    row = lax.broadcasted_iota(jnp.int32, tail.shape, 0)
    return jnp.concatenate(
        [value[: rows - SUBLANES], jnp.where(row == SUBLANES - 1, 0.0, tail)], 0
    )


def position():
    return lax.axis_index("space")


def place(relative, tiles):
    bits = tiles.bit_length() - 1
    return sum((relative >> bit & 1) << (bits - 1 - bit) for bit in range(bits))


def chunks_kernel(own_ref, keep_ref, send_ref):
    frames, rows, _, _ = own_ref.shape
    half = rows // 2
    mine = position() // half
    for out_ref, part in ((keep_ref, mine), (send_ref, 1 - mine)):
        for at in range(half + 2):
            row = part * half + at - 1
            inside = jnp.logical_and(row >= 0, row < rows)
            value = own_ref[:, jnp.clip(row, 0, rows - 1)]
            value = jnp.where(inside, value, jnp.zeros_like(value))
            for pair in range(frames // 2):
                out_ref[0, at, pair] = jnp.concatenate([value[2 * pair], value[2 * pair + 1]], -1)


def halves_kernel(kept_ref, got_ref, keep_ref, send_ref):
    sources = kept_ref.shape[0]
    size = keep_ref.shape[1] - 2
    upper = position() // size % 2
    for at, ref in enumerate((kept_ref, got_ref)):
        to = slice(at * sources, (at + 1) * sources)
        keep_ref[to] = ref[:, pl.ds(upper * size, size + 2)]
        send_ref[to] = ref[:, pl.ds((1 - upper) * size, size + 2)]


def token_weight_kernel(conv_in_ref, token_weight_ref):
    ch = conv_in_ref.shape[3]
    mid = conv_in_ref.shape[4]
    for time in range(3):
        for parity in range(2):
            for near in range(2):
                to = slice(near * mid, (near + 1) * mid)
                for row in range(4):
                    for col in range(4):
                        b = row - near
                        e = col - 1 + parity
                        at = (((col // 2) * 2 + row // 2) * 2 + row % 2) * 2 + col % 2
                        inside = 0 <= b < 3 and 0 <= e < 3
                        token_weight_ref[parity, time, at * ch : (at + 1) * ch, to] = (
                            conv_in_ref[time, b, e] if inside else jnp.zeros((ch, mid), BF16)
                        )


def mixed_kernel(time, conv_mid_ref, mixed_ref, taps, arrived):
    mid = conv_mid_ref.shape[-1]
    parts = arrived.shape[0]
    size = mid // parts
    step = 16

    def spread(g0, g1, g2):
        ends = g0 + g2
        return g0, ends + g1, ends - g1, g2

    def one(i, carry):
        at = pl.ds(pl.multiple_of(i * step, step), step)
        cols = [
            spread(*[taps[b, e, at, :].astype(F32) for b in range(3)]) for e in range(3)
        ]
        for u in range(4):
            for v, value in enumerate(spread(*[cols[e][u] for e in range(3)])):
                mixed_ref[u * 4 + v, at, :] = value.astype(BF16)
        return carry

    copies = []
    for part in range(parts):
        at = pl.ds(part * size, size)
        copies.append(
            pltpu.make_async_copy(
                conv_mid_ref.at[time, :, :, at], taps.at[:, :, at], arrived.at[part]
            )
        )
        copies[-1].start()
    for part in range(parts):
        copies[part].wait()
        lax.fori_loop(part * size // step, (part + 1) * size // step, one, 0)


def windows(ref, first, out, valid=None):
    tiles, _, pairs, cols, pair = ref.shape
    width = pair // 2
    me = position()
    got = [ref[place(tile ^ me, tiles)].astype(F32) for tile in range(tiles)]
    for two in range(pairs):
        line = [jnp.concatenate([value[near, two] for value in got], 0) for near in range(3)]
        if valid is not None:
            line = [jnp.where(valid, value, 0.0) for value in line]
        for half in range(2):
            above, below = line[half], line[half + 1]
            for odd in range(2):
                f = first + 2 * two + odd
                at = slice(odd * width, (odd + 1) * width)
                value = jnp.concatenate([above[:, at], below[:, at]], -1)
                here = value.astype(BF16)
                out[0, half, f] = jnp.concatenate([moved_down(value).astype(BF16), here], -1)
                out[1, half, f] = jnp.concatenate([here, moved_up(value).astype(BF16)], -1)


def stacked(take, frames):
    return jnp.concatenate(
        [jnp.concatenate([take(f + a) for f in frames], 0) for a in range(3)], -1
    )


def activate(take, frames, blank, tiles, weight_ref, in_bias_ref, gain_ref, active, feature, evens=lambda: None):
    mid = gain_ref.shape[0]
    in_bias = in_bias_ref[...].reshape(1, mid)
    half_gain = gain_ref[...].reshape(1, mid) * 0.5
    me = position()
    started = (lax.axis_index("tm") > 0).astype(F32)
    top = (me > 0).astype(F32)
    bottom = (me < tiles - 1).astype(F32)
    for parity in range(2):
        if parity == 1:
            evens()
        weight = weight_ref[parity].reshape(-1, 2 * mid)
        for half in range(2):
            left = stacked(lambda f: take(parity, half, f), frames)
            wide = left.shape[0] // len(frames)
            summed = dot(left, weight)
            for near in range(2):
                row = half * 2 + near
                rounded = (summed[:, near * mid : (near + 1) * mid] + in_bias).astype(BF16)
                if row in (1, 2):
                    feature[row - 1, parity] = rounded[blank * wide :].reshape(-1, wide, mid)
                value = rounded.astype(F32)
                mean = jnp.mean(value * value, axis=-1, keepdims=True)
                scale = lax.rsqrt(mean + 1e-06)
                if row == 0:
                    scale = scale * top
                if row == 3:
                    scale = scale * bottom
                if blank:
                    scale = jnp.concatenate(
                        [scale[: blank * wide] * started, scale[blank * wide :]], 0
                    )
                h = value * scale * half_gain
                active[row, parity] = (
                    (h + h * jnp.tanh(h)).astype(BF16).reshape(len(frames), wide, mid)
                )


def transform(active, f, u, spectrum, parts=range(4)):
    def over_rows(parity):
        r = [active[row, parity, f].astype(F32) for row in ((0, 2), (1, 2), (2, 1), (1, 3))[u]]
        return r[0] + r[1] if u == 1 else r[0] - r[1]

    even = over_rows(0) if set(parts) - {0} else None
    odd = over_rows(1) if set(parts) - {3} else None
    for v in parts:
        if v == 0:
            value = moved_down(odd) - odd
        elif v == 1:
            value = even + odd
        elif v == 2:
            value = odd - even
        else:
            value = even - moved_up(even)
        spectrum[u * 4 + v][f] = value.astype(BF16)


def front_kernel(
    own_ref, token_weight_ref, in_bias_ref, gain_ref, windows_ref, feature_ref, spectrum_ref, active
):
    windows(own_ref, 0, windows_ref)
    activate(
        lambda parity, half, f: windows_ref[parity, half, f],
        range(windows_ref.shape[2] - 2),
        0,
        own_ref.shape[0],
        token_weight_ref,
        in_bias_ref,
        gain_ref,
        active,
        feature_ref,
    )
    parts = [spectrum_ref.at[at] for at in range(16)]
    for u in range(4):
        for f in range(active.shape[2]):
            transform(active, f, u, parts)


def block_kernel(
    previous_ref,
    windows_ref,
    late_feature_ref,
    late_spectrum_ref,
    token_weight_ref,
    in_bias_ref,
    gain_ref,
    mixed_0_ref,
    mixed_1_ref,
    mixed_2_ref,
    mid_bias_ref,
    out_ref,
    early_windows,
    active,
    feature,
    spectrum,
    lines,
    rounded,
    sent,
):
    tiles = previous_ref.shape[0]
    frames, rows, _, mid = out_ref.shape
    held = early_windows.shape[2]
    early = spectrum[0].shape[0]
    late = frames - late_feature_ref.shape[2]
    wide = spectrum[0].shape[1]

    windows(previous_ref, 0, early_windows, lax.axis_index("tm") > 0)
    activate(
        lambda parity, half, f: (
            early_windows[parity, half, f]
            if f < held
            else windows_ref[parity, half, f - held]
        ),
        range(early),
        2,
        tiles,
        token_weight_ref,
        in_bias_ref,
        gain_ref,
        active,
        feature,
        lambda: [transform(active, f, u, spectrum, (3,)) for u in range(4) for f in range(early)],
    )

    def back(m0, m1, m2, m3):
        return m0 + 0.5 * (m1 + m2), 0.5 * (m1 - m2) - m3

    def product(at):
        def take(f):
            return spectrum[at][f] if f < early else late_spectrum_ref[at, f - early]

        right = jnp.concatenate([ref[at] for ref in (mixed_0_ref, mixed_1_ref, mixed_2_ref)], 0)
        left = stacked(take, range(frames))
        return lax.dot_general(right, left, (((0,), (1,)), ((), ())), preferred_element_type=F32)

    mid_bias = mid_bias_ref[...].reshape(1, mid)

    def finish(row, totals):
        for parity in range(2):
            total = (totals[parity].T + mid_bias).reshape(frames, wide, mid)
            for f in range(frames):
                held_feature = (
                    feature[row, parity, f] if f < late else late_feature_ref[row, parity, f - late]
                )
                value = total[f] + held_feature.astype(F32)
                for lane in range(mid // LANES):
                    lines[f, lane, pl.ds(parity, wide, stride=2), :] = value[
                        :, lane * LANES : (lane + 1) * LANES
                    ]
        for f in range(frames):
            for lane in range(mid // LANES):
                rounded[row, f, :, lane * LANES : (lane + 1) * LANES] = lines[f, lane].astype(BF16)
        copy = pltpu.make_async_copy(rounded.at[row], out_ref.at[:, row], sent.at[row])
        copy.start()
        return copy

    def chores(u):
        return [functools.partial(transform, active, f, u, spectrum, (0, 1, 2)) for f in range(early)]

    last = []
    todo = chores(0) + chores(1)
    for u in range(4):
        last.append(product(u * 4 + 3))
        for chore in todo[2 * u : 2 * u + 2]:
            chore()
    sums = []
    copies = []
    for u in range(4):
        todo = chores(u + 2) if u < 2 else []
        parts = []
        for v in range(3):
            parts.append(product(u * 4 + v))
            for chore in todo[v::3]:
                chore()
        sums.append(back(*parts, last[u]))
        if u == 2:
            totals = [sums[0][p] + 0.5 * (sums[1][p] + sums[2][p]) for p in range(2)]
            copies.append(finish(0, totals))
    totals = [0.5 * (sums[1][p] - sums[2][p]) - sums[3][p] for p in range(2)]
    copies.append(finish(1, totals))
    for copy in copies:
        copy.wait()


def limited(mebibytes):
    return pltpu.CompilerParams(vmem_limit_bytes=mebibytes * 2**20)


def after(value, *others):
    return lax.optimization_barrier((value, *others))[0]


def fast(value):
    return pltpu.with_memory_space_constraint(value, pltpu.VMEM)


def far(value):
    return pltpu.with_memory_space_constraint(value, pltpu.HBM)


def exchanged(keep, send, axis, beside):
    count = lax.axis_size(axis)
    size = count // 2
    while True:
        got = lax.ppermute(send, axis, [(one, one ^ size) for one in range(count)])
        done = beside(send)
        if size == 1:
            return after(jnp.concatenate([keep, got], 0), *done)
        size //= 2
        half = jax.ShapeDtypeStruct((2 * keep.shape[0], size + 2, *keep.shape[2:]), keep.dtype)
        keep, send = pl.pallas_call(
            halves_kernel, out_shape=(half, half), compiler_params=limited(2), name="halves"
        )(keep, got)
        send = after(send, *done)


def shifted(value, axis):
    count = lax.axis_size(axis)
    return lax.ppermute(value, axis, [(at, (at + 1) % count) for at in range(count)])


def per_device(
    latent_tokens, conv_in_weight, conv_in_bias, norm_gain, conv_mid_weight, conv_mid_bias
):
    frames, token_rows, cols, width = latent_tokens.shape
    tiles = lax.axis_size("space")
    assert token_rows == tiles and tiles & (tiles - 1) == 0 and frames == 4
    mid = conv_mid_weight.shape[-1]
    wide = tiles * cols
    line = (frames // 2, cols, 2 * width)

    half = jax.ShapeDtypeStruct((1, tiles // 2 + 2) + line, BF16)
    keep, send = pl.pallas_call(chunks_kernel, out_shape=(half, half), compiler_params=limited(2), name="chunks")(
        latent_tokens
    )
    mixed = []

    def beside(value):
        time = len(mixed)
        if time == 3:
            return ()
        weight = far(after(conv_mid_weight, value))
        mixed.append(
            pl.pallas_call(
                functools.partial(mixed_kernel, time),
                out_shape=pltpu.VMEM((16, mid, mid), BF16),
                in_specs=[pl.BlockSpec(memory_space=pltpu.HBM)],
                scratch_shapes=[pltpu.VMEM((3, 3, mid, mid), BF16), pltpu.SemaphoreType.DMA((4,))],
                cost_estimate=pl.CostEstimate(
                    flops=0, bytes_accessed=50 * mid * mid, transcendentals=0
                ),
                compiler_params=limited(6),
                name="mixed",
            )(weight)
        )
        if time < 2:
            return mixed[-1:]
        token_weight.append(
            pl.pallas_call(
                token_weight_kernel,
                out_shape=pltpu.VMEM((2, 3, 4 * width, 2 * mid), BF16),
                cost_estimate=pl.CostEstimate(
                    flops=0, bytes_accessed=4 * 2**20, transcendentals=0
                ),
                compiler_params=limited(4),
                name="token_weight",
            )(conv_in_weight)
        )
        return mixed[-1:] + token_weight

    token_weight = []
    own = exchanged(keep, send, "space", beside)
    while len(mixed) < 3:
        beside(own)
    previous = shifted(own, "tm")

    late = 2
    early = frames + 2 - late
    windows_shape = (2, 2, frames, wide, 4 * width)
    own_windows, late_feature, late_spectrum = pl.pallas_call(
        front_kernel,
        out_shape=(
            pltpu.VMEM(windows_shape, BF16),
            pltpu.VMEM((2, 2, late, wide, mid), BF16),
            pltpu.VMEM((16, late, wide, mid), BF16),
        ),
        scratch_shapes=[pltpu.VMEM((4, 2, late, wide, mid), BF16)],
        cost_estimate=pl.CostEstimate(
            flops=0, bytes_accessed=50 * mid * mid, transcendentals=0
        ),
        compiler_params=limited(8),
        name="front",
    )(own, fast(token_weight[0]), conv_in_bias, norm_gain)

    return pl.pallas_call(
        block_kernel,
        out_shape=jax.ShapeDtypeStruct((frames, 2, 2 * wide, mid), BF16),
        out_specs=pl.BlockSpec(memory_space=pltpu.HBM),
        scratch_shapes=[
            pltpu.VMEM(windows_shape, BF16),
            pltpu.VMEM((4, 2, early, wide, mid), BF16),
            pltpu.VMEM((2, 2, frames - late, wide, mid), BF16),
            [pltpu.VMEM((early, wide, mid), BF16) for _ in range(16)],
            pltpu.VMEM((frames, mid // LANES, 2 * wide, LANES), F32),
            pltpu.VMEM((2, frames, 2 * wide, mid), BF16),
            pltpu.SemaphoreType.DMA((2,)),
        ],
        compiler_params=limited(24),
        name="block",
    )(
        previous,
        fast(own_windows),
        fast(late_feature),
        fast(late_spectrum),
        fast(token_weight[0]),
        conv_in_bias,
        norm_gain,
        *[fast(value) for value in mixed],
        conv_mid_bias,
    )


def solution(mesh):
    return jax.shard_map(
        per_device,
        mesh=mesh,
        in_specs=(P("tm", None, "space", None), P(), P(), P(), P(), P()),
        out_specs=P("tm", "space", None, None),
        check_vma=False,
    )
```

```python
import functools

import jax
import jax.numpy as jnp
from jax import lax
from jax.experimental import pallas as pl
from jax.experimental.pallas import tpu as pltpu
from jax.sharding import PartitionSpec as P

BF16 = jnp.bfloat16
F32 = jnp.float32
LANES = 128
SUBLANES = 8


def dot(left, right):
    return jnp.dot(left, right, preferred_element_type=F32)


def moved_down(value):
    value = pltpu.roll(value, 1, 0)
    head = value[:SUBLANES]
    row = lax.broadcasted_iota(jnp.int32, head.shape, 0)
    return jnp.concatenate([jnp.where(row == 0, 0.0, head), value[SUBLANES:]], 0)


def moved_up(value):
    rows = value.shape[0]
    value = pltpu.roll(value, rows - 1, 0)
    tail = value[rows - SUBLANES :]
    row = lax.broadcasted_iota(jnp.int32, tail.shape, 0)
    return jnp.concatenate(
        [value[: rows - SUBLANES], jnp.where(row == SUBLANES - 1, 0.0, tail)], 0
    )


def position():
    return lax.axis_index("space")


def place(relative, tiles):
    bits = tiles.bit_length() - 1
    return sum((relative >> bit & 1) << (bits - 1 - bit) for bit in range(bits))


def chunks_kernel(own_ref, keep_ref, send_ref):
    frames, rows, _, _ = own_ref.shape
    half = rows // 2
    mine = position() // half
    for out_ref, part in ((keep_ref, mine), (send_ref, 1 - mine)):
        for at in range(half + 2):
            row = part * half + at - 1
            inside = jnp.logical_and(row >= 0, row < rows)
            value = own_ref[:, jnp.clip(row, 0, rows - 1)]
            value = jnp.where(inside, value, jnp.zeros_like(value))
            for pair in range(frames // 2):
                out_ref[0, at, pair] = jnp.concatenate([value[2 * pair], value[2 * pair + 1]], -1)


def halves_kernel(kept_ref, got_ref, keep_ref, send_ref):
    sources = kept_ref.shape[0]
    size = keep_ref.shape[1] - 2
    upper = position() // size % 2
    for at, ref in enumerate((kept_ref, got_ref)):
        to = slice(at * sources, (at + 1) * sources)
        keep_ref[to] = ref[:, pl.ds(upper * size, size + 2)]
        send_ref[to] = ref[:, pl.ds((1 - upper) * size, size + 2)]


def token_weight_kernel(conv_in_ref, token_weight_ref):
    ch = conv_in_ref.shape[3]
    mid = conv_in_ref.shape[4]
    for time in range(3):
        for parity in range(2):
            for near in range(2):
                to = slice(near * mid, (near + 1) * mid)
                for row in range(4):
                    for col in range(4):
                        b = row - near
                        e = col - 1 + parity
                        at = (((col // 2) * 2 + row // 2) * 2 + row % 2) * 2 + col % 2
                        inside = 0 <= b < 3 and 0 <= e < 3
                        token_weight_ref[parity, time, at * ch : (at + 1) * ch, to] = (
                            conv_in_ref[time, b, e] if inside else jnp.zeros((ch, mid), BF16)
                        )


def mixed_kernel(time, conv_mid_ref, mixed_ref, taps, arrived):
    mid = conv_mid_ref.shape[-1]
    parts = arrived.shape[0]
    size = mid // parts
    step = 16

    def spread(g0, g1, g2):
        ends = g0 + g2
        return g0, ends + g1, ends - g1, g2

    def one(i, carry):
        at = pl.ds(pl.multiple_of(i * step, step), step)
        cols = [
            spread(*[taps[b, e, at, :].astype(F32) for b in range(3)]) for e in range(3)
        ]
        for u in range(4):
            for v, value in enumerate(spread(*[cols[e][u] for e in range(3)])):
                mixed_ref[u * 4 + v, at, :] = value.astype(BF16)
        return carry

    copies = []
    for part in range(parts):
        at = pl.ds(part * size, size)
        copies.append(
            pltpu.make_async_copy(
                conv_mid_ref.at[time, :, :, at], taps.at[:, :, at], arrived.at[part]
            )
        )
        copies[-1].start()
    for part in range(parts):
        copies[part].wait()
        lax.fori_loop(part * size // step, (part + 1) * size // step, one, 0)


def windows(ref, first, out):
    tiles, _, pairs, cols, pair = ref.shape
    width = pair // 2
    me = position()
    got = [ref[place(tile ^ me, tiles)].astype(F32) for tile in range(tiles)]
    for two in range(pairs):
        line = [jnp.concatenate([value[near, two] for value in got], 0) for near in range(3)]
        for half in range(2):
            above, below = line[half], line[half + 1]
            for odd in range(2):
                f = first + 2 * two + odd
                at = slice(odd * width, (odd + 1) * width)
                value = jnp.concatenate([above[:, at], below[:, at]], -1)
                here = value.astype(BF16)
                out[0, half, f] = jnp.concatenate([moved_down(value).astype(BF16), here], -1)
                out[1, half, f] = jnp.concatenate([here, moved_up(value).astype(BF16)], -1)


def stacked(take, frames):
    return jnp.concatenate(
        [jnp.concatenate([take(f + a) for f in frames], 0) for a in range(3)], -1
    )


def activate(take, frames, skip, tiles, weight_ref, in_bias_ref, gain_ref, active, feature, evens=lambda: None):
    mid = gain_ref.shape[0]
    in_bias = in_bias_ref[...].reshape(1, mid)
    half_gain = gain_ref[...].reshape(1, mid) * 0.5
    me = position()
    top = (me > 0).astype(F32)
    bottom = (me < tiles - 1).astype(F32)
    for parity in range(2):
        if parity == 1:
            evens()
        weight = weight_ref[parity].reshape(-1, 2 * mid)
        for half in range(2):
            left = stacked(lambda f: take(parity, half, f), frames)
            wide = left.shape[0] // len(frames)
            summed = dot(left, weight)
            for near in range(2):
                row = half * 2 + near
                rounded = (summed[:, near * mid : (near + 1) * mid] + in_bias).astype(BF16)
                if row in (1, 2):
                    feature[row - 1, parity] = rounded[skip * wide :].reshape(-1, wide, mid)
                value = rounded.astype(F32)
                mean = jnp.mean(value * value, axis=-1, keepdims=True)
                scale = lax.rsqrt(mean + 1e-06)
                if row == 0:
                    scale = scale * top
                if row == 3:
                    scale = scale * bottom
                h = value * scale * half_gain
                active[row, parity, frames.start : frames.stop] = (
                    (h + h * jnp.tanh(h)).astype(BF16).reshape(len(frames), wide, mid)
                )


def transform(active, f, u, spectrum, parts=range(4)):
    def over_rows(parity):
        r = [active[row, parity, f].astype(F32) for row in ((0, 2), (1, 2), (2, 1), (1, 3))[u]]
        return r[0] + r[1] if u == 1 else r[0] - r[1]

    even = over_rows(0) if set(parts) - {0} else None
    odd = over_rows(1) if set(parts) - {3} else None
    for v in parts:
        if v == 0:
            value = moved_down(odd) - odd
        elif v == 1:
            value = even + odd
        elif v == 2:
            value = odd - even
        else:
            value = even - moved_up(even)
        spectrum[u * 4 + v][f] = value.astype(BF16)


def front_kernel(
    own_ref, token_weight_ref, in_bias_ref, gain_ref, windows_ref, feature_ref, spectrum_ref, active
):
    windows(own_ref, 0, windows_ref)
    activate(
        lambda parity, half, f: windows_ref[parity, half, f],
        range(windows_ref.shape[2] - 2),
        0,
        own_ref.shape[0],
        token_weight_ref,
        in_bias_ref,
        gain_ref,
        active,
        feature_ref,
    )
    parts = [spectrum_ref.at[at] for at in range(16)]
    for u in range(4):
        for f in range(active.shape[2]):
            transform(active, f, u, parts)


def block_kernel(
    previous_ref,
    windows_ref,
    late_feature_ref,
    late_spectrum_ref,
    token_weight_ref,
    in_bias_ref,
    gain_ref,
    mixed_0_ref,
    mixed_1_ref,
    mixed_2_ref,
    mid_bias_ref,
    out_ref,
    early_windows,
    active,
    feature,
    spectrum,
    lines,
    rounded,
    sent,
):
    tiles = previous_ref.shape[0]
    frames, rows, _, mid = out_ref.shape
    held = early_windows.shape[2]
    early = spectrum[0].shape[0]
    late = frames - late_feature_ref.shape[2]
    wide = spectrum[0].shape[1]

    def run(start):
        if start == 0:
            windows(previous_ref, 0, early_windows)

        def window(parity, half, f):
            if f >= held:
                return windows_ref[parity, half, f - held]
            if start:
                return jnp.zeros(early_windows.shape[3:], BF16)
            return early_windows[parity, half, f]

        activate(
            window,
            range(start, early),
            2 - start,
            tiles,
            token_weight_ref,
            in_bias_ref,
            gain_ref,
            active,
            feature,
            lambda: [
                transform(active, f, u, spectrum, (3,)) for u in range(4) for f in range(start, early)
            ],
        )

        def back(m0, m1, m2, m3):
            return m0 + 0.5 * (m1 + m2), 0.5 * (m1 - m2) - m3

        def product(at):
            def take(f):
                if f < start:
                    return jnp.zeros((wide, mid), BF16)
                return spectrum[at][f] if f < early else late_spectrum_ref[at, f - early]

            right = jnp.concatenate([ref[at] for ref in (mixed_0_ref, mixed_1_ref, mixed_2_ref)], 0)
            left = stacked(take, range(frames))
            return lax.dot_general(right, left, (((0,), (1,)), ((), ())), preferred_element_type=F32)

        mid_bias = mid_bias_ref[...].reshape(1, mid)

        def finish(row, totals):
            for parity in range(2):
                total = (totals[parity].T + mid_bias).reshape(frames, wide, mid)
                for f in range(frames):
                    held_feature = (
                        feature[row, parity, f] if f < late else late_feature_ref[row, parity, f - late]
                    )
                    value = total[f] + held_feature.astype(F32)
                    for lane in range(mid // LANES):
                        lines[f, lane, pl.ds(parity, wide, stride=2), :] = value[
                            :, lane * LANES : (lane + 1) * LANES
                        ]
            for f in range(frames):
                for lane in range(mid // LANES):
                    rounded[row, f, :, lane * LANES : (lane + 1) * LANES] = lines[f, lane].astype(BF16)
            copy = pltpu.make_async_copy(rounded.at[row], out_ref.at[:, row], sent.at[row])
            copy.start()
            return copy

        def chores(u):
            return [functools.partial(transform, active, f, u, spectrum, (0, 1, 2)) for f in range(start, early)]

        last = []
        todo = chores(0) + chores(1)
        for u in range(4):
            last.append(product(u * 4 + 3))
            for chore in todo[u::4]:
                chore()
        sums = []
        copies = []
        for u in range(4):
            todo = chores(u + 2) if u < 2 else []
            parts = []
            for v in range(3):
                parts.append(product(u * 4 + v))
                for chore in todo[v::3]:
                    chore()
            sums.append(back(*parts, last[u]))
            if u == 2:
                totals = [sums[0][p] + 0.5 * (sums[1][p] + sums[2][p]) for p in range(2)]
                copies.append(finish(0, totals))
        totals = [0.5 * (sums[1][p] - sums[2][p]) - sums[3][p] for p in range(2)]
        copies.append(finish(1, totals))
        for copy in copies:
            copy.wait()

    pl.when(lax.axis_index("tm") > 0)(lambda: run(0))
    pl.when(lax.axis_index("tm") == 0)(lambda: run(2))


def limited(mebibytes):
    return pltpu.CompilerParams(vmem_limit_bytes=mebibytes * 2**20)


def after(value, *others):
    return lax.optimization_barrier((value, *others))[0]


def fast(value):
    return pltpu.with_memory_space_constraint(value, pltpu.VMEM)


def far(value):
    return pltpu.with_memory_space_constraint(value, pltpu.HBM)


def exchanged(keep, send, axis, beside):
    count = lax.axis_size(axis)
    size = count // 2
    while True:
        got = lax.ppermute(send, axis, [(one, one ^ size) for one in range(count)])
        done = beside(send)
        if size == 1:
            return after(jnp.concatenate([keep, got], 0), *done)
        size //= 2
        half = jax.ShapeDtypeStruct((2 * keep.shape[0], size + 2, *keep.shape[2:]), keep.dtype)
        keep, send = pl.pallas_call(
            halves_kernel, out_shape=(half, half), compiler_params=limited(2), name="halves"
        )(keep, got)
        send = after(send, *done)


def shifted(value, axis):
    count = lax.axis_size(axis)
    return lax.ppermute(value, axis, [(at, (at + 1) % count) for at in range(count)])


def per_device(
    latent_tokens, conv_in_weight, conv_in_bias, norm_gain, conv_mid_weight, conv_mid_bias
):
    frames, token_rows, cols, width = latent_tokens.shape
    tiles = lax.axis_size("space")
    assert token_rows == tiles and tiles & (tiles - 1) == 0 and frames == 4
    mid = conv_mid_weight.shape[-1]
    wide = tiles * cols
    line = (frames // 2, cols, 2 * width)

    half = jax.ShapeDtypeStruct((1, tiles // 2 + 2) + line, BF16)
    keep, send = pl.pallas_call(chunks_kernel, out_shape=(half, half), compiler_params=limited(2), name="chunks")(
        latent_tokens
    )
    mixed = []

    def beside(value):
        time = len(mixed)
        if time == 3:
            return ()
        weight = far(after(conv_mid_weight, value))
        mixed.append(
            pl.pallas_call(
                functools.partial(mixed_kernel, time),
                out_shape=pltpu.VMEM((16, mid, mid), BF16),
                in_specs=[pl.BlockSpec(memory_space=pltpu.HBM)],
                scratch_shapes=[pltpu.VMEM((3, 3, mid, mid), BF16), pltpu.SemaphoreType.DMA((4,))],
                cost_estimate=pl.CostEstimate(
                    flops=0, bytes_accessed=50 * mid * mid, transcendentals=0
                ),
                compiler_params=limited(6),
                name="mixed",
            )(weight)
        )
        if time < 2:
            return mixed[-1:]
        token_weight.append(
            pl.pallas_call(
                token_weight_kernel,
                out_shape=pltpu.VMEM((2, 3, 4 * width, 2 * mid), BF16),
                cost_estimate=pl.CostEstimate(
                    flops=0, bytes_accessed=4 * 2**20, transcendentals=0
                ),
                compiler_params=limited(4),
                name="token_weight",
            )(conv_in_weight)
        )
        return mixed[-1:] + token_weight

    token_weight = []
    own = exchanged(keep, send, "space", beside)
    while len(mixed) < 3:
        beside(own)
    previous = shifted(own, "tm")

    late = 2
    early = frames + 2 - late
    windows_shape = (2, 2, frames, wide, 4 * width)
    own_windows, late_feature, late_spectrum = pl.pallas_call(
        front_kernel,
        out_shape=(
            pltpu.VMEM(windows_shape, BF16),
            pltpu.VMEM((2, 2, late, wide, mid), BF16),
            pltpu.VMEM((16, late, wide, mid), BF16),
        ),
        scratch_shapes=[pltpu.VMEM((4, 2, late, wide, mid), BF16)],
        cost_estimate=pl.CostEstimate(
            flops=0, bytes_accessed=50 * mid * mid, transcendentals=0
        ),
        compiler_params=limited(8),
        name="front",
    )(own, fast(token_weight[0]), conv_in_bias, norm_gain)

    return pl.pallas_call(
        block_kernel,
        out_shape=jax.ShapeDtypeStruct((frames, 2, 2 * wide, mid), BF16),
        out_specs=pl.BlockSpec(memory_space=pltpu.HBM),
        scratch_shapes=[
            pltpu.VMEM(windows_shape, BF16),
            pltpu.VMEM((4, 2, early, wide, mid), BF16),
            pltpu.VMEM((2, 2, frames - late, wide, mid), BF16),
            [pltpu.VMEM((early, wide, mid), BF16) for _ in range(16)],
            pltpu.VMEM((frames, mid // LANES, 2 * wide, LANES), F32),
            pltpu.VMEM((2, frames, 2 * wide, mid), BF16),
            pltpu.SemaphoreType.DMA((2,)),
        ],
        compiler_params=limited(24),
        name="block",
    )(
        previous,
        fast(own_windows),
        fast(late_feature),
        fast(late_spectrum),
        fast(token_weight[0]),
        conv_in_bias,
        norm_gain,
        *[fast(value) for value in mixed],
        conv_mid_bias,
    )


def solution(mesh):
    return jax.shard_map(
        per_device,
        mesh=mesh,
        in_specs=(P("tm", None, "space", None), P(), P(), P(), P(), P()),
        out_specs=P("tm", "space", None, None),
        check_vma=False,
    )
```

```python
import functools

import jax
import jax.numpy as jnp
from jax import lax
from jax.experimental import pallas as pl
from jax.experimental.pallas import tpu as pltpu
from jax.sharding import PartitionSpec as P

BF16 = jnp.bfloat16
F32 = jnp.float32
LANES = 128
SUBLANES = 8


def dot(left, right):
    return jnp.dot(left, right, preferred_element_type=F32)


def moved_down(value):
    value = pltpu.roll(value, 1, 0)
    head = value[:SUBLANES]
    row = lax.broadcasted_iota(jnp.int32, head.shape, 0)
    return jnp.concatenate([jnp.where(row == 0, 0.0, head), value[SUBLANES:]], 0)


def moved_up(value):
    rows = value.shape[0]
    value = pltpu.roll(value, rows - 1, 0)
    tail = value[rows - SUBLANES :]
    row = lax.broadcasted_iota(jnp.int32, tail.shape, 0)
    return jnp.concatenate(
        [value[: rows - SUBLANES], jnp.where(row == SUBLANES - 1, 0.0, tail)], 0
    )


def position():
    return lax.axis_index("space")


def place(relative, tiles):
    bits = tiles.bit_length() - 1
    return sum((relative >> bit & 1) << (bits - 1 - bit) for bit in range(bits))


def chunks_kernel(own_ref, keep_ref, send_ref):
    frames, rows, _, _ = own_ref.shape
    half = rows // 2
    mine = position() // half
    for out_ref, part in ((keep_ref, mine), (send_ref, 1 - mine)):
        for at in range(half + 2):
            row = part * half + at - 1
            inside = jnp.logical_and(row >= 0, row < rows)
            value = own_ref[:, jnp.clip(row, 0, rows - 1)]
            value = jnp.where(inside, value, jnp.zeros_like(value))
            for pair in range(frames // 2):
                out_ref[0, at, pair] = jnp.concatenate([value[2 * pair], value[2 * pair + 1]], -1)


def halves_kernel(kept_ref, got_ref, keep_ref, send_ref):
    sources = kept_ref.shape[0]
    size = keep_ref.shape[1] - 2
    upper = position() // size % 2
    for at, ref in enumerate((kept_ref, got_ref)):
        to = slice(at * sources, (at + 1) * sources)
        keep_ref[to] = ref[:, pl.ds(upper * size, size + 2)]
        send_ref[to] = ref[:, pl.ds((1 - upper) * size, size + 2)]


def token_weight_kernel(conv_in_ref, token_weight_ref):
    ch = conv_in_ref.shape[3]
    mid = conv_in_ref.shape[4]
    for time in range(3):
        for parity in range(2):
            for near in range(2):
                to = slice(near * mid, (near + 1) * mid)
                for row in range(4):
                    for col in range(4):
                        b = row - near
                        e = col - 1 + parity
                        at = (((col // 2) * 2 + row // 2) * 2 + row % 2) * 2 + col % 2
                        inside = 0 <= b < 3 and 0 <= e < 3
                        token_weight_ref[parity, time, at * ch : (at + 1) * ch, to] = (
                            conv_in_ref[time, b, e] if inside else jnp.zeros((ch, mid), BF16)
                        )


def mixed_kernel(time, conv_mid_ref, mixed_ref, taps, arrived):
    mid = conv_mid_ref.shape[-1]
    parts = arrived.shape[0]
    size = mid // parts
    step = 16

    def spread(g0, g1, g2):
        ends = g0 + g2
        return g0, ends + g1, ends - g1, g2

    def one(i, carry):
        at = pl.ds(pl.multiple_of(i * step, step), step)
        cols = [
            spread(*[taps[b, e, at, :].astype(F32) for b in range(3)]) for e in range(3)
        ]
        for u in range(4):
            for v, value in enumerate(spread(*[cols[e][u] for e in range(3)])):
                mixed_ref[u * 4 + v, at, :] = value.astype(BF16)
        return carry

    copies = []
    for part in range(parts):
        at = pl.ds(part * size, size)
        copies.append(
            pltpu.make_async_copy(
                conv_mid_ref.at[time, :, :, at], taps.at[:, :, at], arrived.at[part]
            )
        )
        copies[-1].start()
    for part in range(parts):
        copies[part].wait()
        lax.fori_loop(part * size // step, (part + 1) * size // step, one, 0)


def windows(ref, first, out):
    tiles, _, pairs, cols, pair = ref.shape
    width = pair // 2
    me = position()
    got = [ref[place(tile ^ me, tiles)].astype(F32) for tile in range(tiles)]
    for two in range(pairs):
        line = [jnp.concatenate([value[near, two] for value in got], 0) for near in range(3)]
        for half in range(2):
            above, below = line[half], line[half + 1]
            for odd in range(2):
                f = first + 2 * two + odd
                at = slice(odd * width, (odd + 1) * width)
                value = jnp.concatenate([above[:, at], below[:, at]], -1)
                here = value.astype(BF16)
                out[0, half, f] = jnp.concatenate([moved_down(value).astype(BF16), here], -1)
                out[1, half, f] = jnp.concatenate([here, moved_up(value).astype(BF16)], -1)


def stacked(take, frames):
    return jnp.concatenate(
        [jnp.concatenate([take(f + a) for f in frames], 0) for a in range(3)], -1
    )


def activate(take, frames, skip, tiles, weight_ref, in_bias_ref, gain_ref, active, feature, evens=lambda: None):
    mid = gain_ref.shape[0]
    in_bias = in_bias_ref[...].reshape(1, mid)
    half_gain = gain_ref[...].reshape(1, mid) * 0.5
    me = position()
    top = (me > 0).astype(F32)
    bottom = (me < tiles - 1).astype(F32)
    for parity in range(2):
        if parity == 1:
            evens()
        weight = weight_ref[parity].reshape(-1, 2 * mid)
        for half in range(2):
            left = stacked(lambda f: take(parity, half, f), frames)
            wide = left.shape[0] // len(frames)
            summed = dot(left, weight)
            for near in range(2):
                row = half * 2 + near
                rounded = (summed[:, near * mid : (near + 1) * mid] + in_bias).astype(BF16)
                if row in (1, 2):
                    feature[row - 1, parity] = rounded[skip * wide :].reshape(-1, wide, mid)
                value = rounded.astype(F32)
                mean = jnp.mean(value * value, axis=-1, keepdims=True)
                scale = lax.rsqrt(mean + 1e-06)
                if row == 0:
                    scale = scale * top
                if row == 3:
                    scale = scale * bottom
                h = value * scale * half_gain
                active[row, parity, frames.start : frames.stop] = (
                    (h + h * jnp.tanh(h)).astype(BF16).reshape(len(frames), wide, mid)
                )


def transform(active, f, u, spectrum, parts=range(4)):
    def over_rows(parity):
        r = [active[row, parity, f].astype(F32) for row in ((0, 2), (1, 2), (2, 1), (1, 3))[u]]
        return r[0] + r[1] if u == 1 else r[0] - r[1]

    even = over_rows(0) if set(parts) - {0} else None
    odd = over_rows(1) if set(parts) - {3} else None
    for v in parts:
        if v == 0:
            value = moved_down(odd) - odd
        elif v == 1:
            value = even + odd
        elif v == 2:
            value = odd - even
        else:
            value = even - moved_up(even)
        spectrum[u * 4 + v][f] = value.astype(BF16)


def front_kernel(
    own_ref, token_weight_ref, in_bias_ref, gain_ref, windows_ref, feature_ref, spectrum_ref, active
):
    windows(own_ref, 0, windows_ref)
    activate(
        lambda parity, half, f: windows_ref[parity, half, f],
        range(windows_ref.shape[2] - 2),
        0,
        own_ref.shape[0],
        token_weight_ref,
        in_bias_ref,
        gain_ref,
        active,
        feature_ref,
    )
    parts = [spectrum_ref.at[at] for at in range(16)]
    for u in range(4):
        for f in range(active.shape[2]):
            transform(active, f, u, parts)


def block_kernel(
    previous_ref,
    windows_ref,
    late_feature_ref,
    late_spectrum_ref,
    token_weight_ref,
    in_bias_ref,
    gain_ref,
    mixed_0_ref,
    mixed_1_ref,
    mixed_2_ref,
    mid_bias_ref,
    out_ref,
    early_windows,
    active,
    feature,
    spectrum,
    lines,
    rounded,
    sent,
):
    tiles = previous_ref.shape[0]
    frames, rows, _, mid = out_ref.shape
    held = early_windows.shape[2]
    early = spectrum[0].shape[0]
    late = frames - late_feature_ref.shape[2]
    wide = spectrum[0].shape[1]

    def run(start):
        if start == 0:
            windows(previous_ref, 0, early_windows)

        def window(parity, half, f):
            if f >= held:
                return windows_ref[parity, half, f - held]
            if start:
                return jnp.zeros(early_windows.shape[3:], BF16)
            return early_windows[parity, half, f]

        activate(
            window,
            range(start, early),
            2 - start,
            tiles,
            token_weight_ref,
            in_bias_ref,
            gain_ref,
            active,
            feature,
            lambda: [
                transform(active, f, u, spectrum, (3,)) for u in range(4) for f in range(start, early)
            ],
        )

        def back(m0, m1, m2, m3):
            return m0 + 0.5 * (m1 + m2), 0.5 * (m1 - m2) - m3

        def product(at):
            def take(f):
                if f < start:
                    return jnp.zeros((wide, mid), BF16)
                return spectrum[at][f] if f < early else late_spectrum_ref[at, f - early]

            right = jnp.concatenate([ref[at] for ref in (mixed_0_ref, mixed_1_ref, mixed_2_ref)], 0)
            left = stacked(take, range(frames))
            return lax.dot_general(right, left, (((0,), (1,)), ((), ())), preferred_element_type=F32)

        mid_bias = mid_bias_ref[...].reshape(1, mid)

        def finish(row, totals):
            for parity in range(2):
                total = (totals[parity].T + mid_bias).reshape(frames, wide, mid)
                for f in range(frames):
                    held_feature = (
                        feature[row, parity, f] if f < late else late_feature_ref[row, parity, f - late]
                    )
                    value = total[f] + held_feature.astype(F32)
                    for lane in range(mid // LANES):
                        lines[f, lane, pl.ds(parity, wide, stride=2), :] = value[
                            :, lane * LANES : (lane + 1) * LANES
                        ]
            for f in range(frames):
                for lane in range(mid // LANES):
                    rounded[row, f, :, lane * LANES : (lane + 1) * LANES] = lines[
                        f, lane, : 2 * wide
                    ].astype(BF16)
            copy = pltpu.make_async_copy(rounded.at[row], out_ref.at[:, row], sent.at[row])
            copy.start()
            return copy

        def chores(u):
            return [functools.partial(transform, active, f, u, spectrum, (0, 1, 2)) for f in range(start, early)]

        last = []
        todo = chores(0) + chores(1)
        for u in range(4):
            last.append(product(u * 4 + 3))
            for chore in todo[u::4]:
                chore()
        sums = []
        copies = []
        for u in range(4):
            todo = chores(u + 2) if u < 2 else []
            parts = []
            for v in range(3):
                parts.append(product(u * 4 + v))
                for chore in todo[v::3]:
                    chore()
            sums.append(back(*parts, last[u]))
            if u == 2:
                totals = [sums[0][p] + 0.5 * (sums[1][p] + sums[2][p]) for p in range(2)]
                copies.append(finish(0, totals))
        totals = [0.5 * (sums[1][p] - sums[2][p]) - sums[3][p] for p in range(2)]
        copies.append(finish(1, totals))
        for copy in copies:
            copy.wait()

    pl.when(lax.axis_index("tm") > 0)(lambda: run(0))
    pl.when(lax.axis_index("tm") == 0)(lambda: run(2))


def limited(mebibytes):
    return pltpu.CompilerParams(vmem_limit_bytes=mebibytes * 2**20)


def after(value, *others):
    return lax.optimization_barrier((value, *others))[0]


def fast(value):
    return pltpu.with_memory_space_constraint(value, pltpu.VMEM)


def far(value):
    return pltpu.with_memory_space_constraint(value, pltpu.HBM)


def exchanged(keep, send, axis, beside):
    count = lax.axis_size(axis)
    size = count // 2
    while True:
        got = lax.ppermute(send, axis, [(one, one ^ size) for one in range(count)])
        done = beside(send)
        if size == 1:
            return after(jnp.concatenate([keep, got], 0), *done)
        size //= 2
        half = jax.ShapeDtypeStruct((2 * keep.shape[0], size + 2, *keep.shape[2:]), keep.dtype)
        keep, send = pl.pallas_call(
            halves_kernel, out_shape=(half, half), compiler_params=limited(2), name="halves"
        )(keep, got)
        send = after(send, *done)


def shifted(value, axis):
    count = lax.axis_size(axis)
    return lax.ppermute(value, axis, [(at, (at + 1) % count) for at in range(count)])


def per_device(
    latent_tokens, conv_in_weight, conv_in_bias, norm_gain, conv_mid_weight, conv_mid_bias
):
    frames, token_rows, cols, width = latent_tokens.shape
    tiles = lax.axis_size("space")
    assert token_rows == tiles and tiles & (tiles - 1) == 0 and frames == 4
    mid = conv_mid_weight.shape[-1]
    wide = tiles * cols
    line = (frames // 2, cols, 2 * width)

    half = jax.ShapeDtypeStruct((1, tiles // 2 + 2) + line, BF16)
    keep, send = pl.pallas_call(chunks_kernel, out_shape=(half, half), compiler_params=limited(2), name="chunks")(
        latent_tokens
    )
    mixed = []

    def beside(value):
        time = len(mixed)
        if time == 3:
            return ()
        weight = far(after(conv_mid_weight, value))
        mixed.append(
            pl.pallas_call(
                functools.partial(mixed_kernel, time),
                out_shape=pltpu.VMEM((16, mid, mid), BF16),
                in_specs=[pl.BlockSpec(memory_space=pltpu.HBM)],
                scratch_shapes=[pltpu.VMEM((3, 3, mid, mid), BF16), pltpu.SemaphoreType.DMA((4,))],
                cost_estimate=pl.CostEstimate(
                    flops=0, bytes_accessed=50 * mid * mid, transcendentals=0
                ),
                compiler_params=limited(6),
                name="mixed",
            )(weight)
        )
        if time < 2:
            return mixed[-1:]
        token_weight.append(
            pl.pallas_call(
                token_weight_kernel,
                out_shape=pltpu.VMEM((2, 3, 4 * width, 2 * mid), BF16),
                cost_estimate=pl.CostEstimate(
                    flops=0, bytes_accessed=4 * 2**20, transcendentals=0
                ),
                compiler_params=limited(4),
                name="token_weight",
            )(conv_in_weight)
        )
        return mixed[-1:] + token_weight

    token_weight = []
    own = exchanged(keep, send, "space", beside)
    while len(mixed) < 3:
        beside(own)
    previous = shifted(own, "tm")

    late = 2
    early = frames + 2 - late
    windows_shape = (2, 2, frames, wide, 4 * width)
    own_windows, late_feature, late_spectrum = pl.pallas_call(
        front_kernel,
        out_shape=(
            pltpu.VMEM(windows_shape, BF16),
            pltpu.VMEM((2, 2, late, wide, mid), BF16),
            pltpu.VMEM((16, late, wide, mid), BF16),
        ),
        scratch_shapes=[pltpu.VMEM((4, 2, late, wide, mid), BF16)],
        cost_estimate=pl.CostEstimate(
            flops=0, bytes_accessed=50 * mid * mid, transcendentals=0
        ),
        compiler_params=limited(8),
        name="front",
    )(own, fast(token_weight[0]), conv_in_bias, norm_gain)

    return pl.pallas_call(
        block_kernel,
        out_shape=jax.ShapeDtypeStruct((frames, 2, 2 * wide, mid), BF16),
        out_specs=pl.BlockSpec(memory_space=pltpu.HBM),
        scratch_shapes=[
            pltpu.VMEM(windows_shape, BF16),
            pltpu.VMEM((4, 2, early, wide, mid), BF16),
            pltpu.VMEM((2, 2, frames - late, wide, mid), BF16),
            [pltpu.VMEM((early, wide, mid), BF16) for _ in range(16)],
            pltpu.VMEM((frames, mid // LANES, 2 * wide + SUBLANES, LANES), F32),
            pltpu.VMEM((2, frames, 2 * wide, mid), BF16),
            pltpu.SemaphoreType.DMA((2,)),
        ],
        compiler_params=limited(24),
        name="block",
    )(
        previous,
        fast(own_windows),
        fast(late_feature),
        fast(late_spectrum),
        fast(token_weight[0]),
        conv_in_bias,
        norm_gain,
        *[fast(value) for value in mixed],
        conv_mid_bias,
    )


def solution(mesh):
    return jax.shard_map(
        per_device,
        mesh=mesh,
        in_specs=(P("tm", None, "space", None), P(), P(), P(), P(), P()),
        out_specs=P("tm", "space", None, None),
        check_vma=False,
    )
```

```python
import functools

import jax
import jax.numpy as jnp
from jax import lax
from jax.experimental import pallas as pl
from jax.experimental.pallas import tpu as pltpu
from jax.sharding import PartitionSpec as P

BF16 = jnp.bfloat16
F32 = jnp.float32
LANES = 128
SUBLANES = 8


def dot(left, right):
    return jnp.dot(left, right, preferred_element_type=F32)


def moved_down(value):
    value = pltpu.roll(value, 1, 0)
    head = value[:SUBLANES]
    row = lax.broadcasted_iota(jnp.int32, head.shape, 0)
    return jnp.concatenate([jnp.where(row == 0, 0.0, head), value[SUBLANES:]], 0)


def moved_up(value):
    rows = value.shape[0]
    value = pltpu.roll(value, rows - 1, 0)
    tail = value[rows - SUBLANES :]
    row = lax.broadcasted_iota(jnp.int32, tail.shape, 0)
    return jnp.concatenate(
        [value[: rows - SUBLANES], jnp.where(row == SUBLANES - 1, 0.0, tail)], 0
    )


def position():
    return lax.axis_index("space")


def place(relative, tiles):
    bits = tiles.bit_length() - 1
    return sum((relative >> bit & 1) << (bits - 1 - bit) for bit in range(bits))


def chunks_kernel(tokens_ref, keep_ref, send_ref, own_ref, arrived):
    frames, rows, _, _ = own_ref.shape
    copies = [
        pltpu.make_async_copy(tokens_ref.at[f], own_ref.at[f], arrived.at[f]) for f in range(frames)
    ]
    for copy in copies:
        copy.start()
    half = rows // 2
    mine = position() // half
    for copy in copies:
        copy.wait()
    for out_ref, part in ((keep_ref, mine), (send_ref, 1 - mine)):
        for at in range(half + 2):
            row = part * half + at - 1
            inside = jnp.logical_and(row >= 0, row < rows)
            value = own_ref[:, jnp.clip(row, 0, rows - 1)]
            value = jnp.where(inside, value, jnp.zeros_like(value))
            for pair in range(frames // 2):
                out_ref[0, at, pair] = jnp.concatenate([value[2 * pair], value[2 * pair + 1]], -1)


def halves_kernel(kept_ref, got_ref, keep_ref, send_ref):
    sources = kept_ref.shape[0]
    size = keep_ref.shape[1] - 2
    upper = position() // size % 2
    for at, ref in enumerate((kept_ref, got_ref)):
        to = slice(at * sources, (at + 1) * sources)
        keep_ref[to] = ref[:, pl.ds(upper * size, size + 2)]
        send_ref[to] = ref[:, pl.ds((1 - upper) * size, size + 2)]


def token_weight_kernel(conv_in_ref, token_weight_ref):
    ch = conv_in_ref.shape[3]
    mid = conv_in_ref.shape[4]
    for time in range(3):
        for parity in range(2):
            for near in range(2):
                to = slice(near * mid, (near + 1) * mid)
                for row in range(4):
                    for col in range(4):
                        b = row - near
                        e = col - 1 + parity
                        at = (((col // 2) * 2 + row // 2) * 2 + row % 2) * 2 + col % 2
                        inside = 0 <= b < 3 and 0 <= e < 3
                        token_weight_ref[parity, time, at * ch : (at + 1) * ch, to] = (
                            conv_in_ref[time, b, e] if inside else jnp.zeros((ch, mid), BF16)
                        )


def mixed_kernel(time, conv_mid_ref, mixed_ref, taps, arrived):
    mid = conv_mid_ref.shape[-1]
    parts = arrived.shape[0]
    size = mid // parts
    step = 16

    def spread(g0, g1, g2):
        ends = g0 + g2
        return g0, ends + g1, ends - g1, g2

    def one(i, carry):
        at = pl.ds(pl.multiple_of(i * step, step), step)
        cols = [
            spread(*[taps[b, e, at, :].astype(F32) for b in range(3)]) for e in range(3)
        ]
        for u in range(4):
            for v, value in enumerate(spread(*[cols[e][u] for e in range(3)])):
                mixed_ref[u * 4 + v, at, :] = value.astype(BF16)
        return carry

    copies = []
    for part in range(parts):
        at = pl.ds(part * size, size)
        copies.append(
            pltpu.make_async_copy(
                conv_mid_ref.at[time, :, :, at], taps.at[:, :, at], arrived.at[part]
            )
        )
        copies[-1].start()
    for part in range(parts):
        copies[part].wait()
        lax.fori_loop(part * size // step, (part + 1) * size // step, one, 0)


def windows(ref, first, out):
    tiles, _, pairs, cols, pair = ref.shape
    width = pair // 2
    me = position()
    got = [ref[place(tile ^ me, tiles)].astype(F32) for tile in range(tiles)]
    for two in range(pairs):
        line = [jnp.concatenate([value[near, two] for value in got], 0) for near in range(3)]
        for half in range(2):
            above, below = line[half], line[half + 1]
            for odd in range(2):
                f = first + 2 * two + odd
                at = slice(odd * width, (odd + 1) * width)
                value = jnp.concatenate([above[:, at], below[:, at]], -1)
                here = value.astype(BF16)
                out[0, half, f] = jnp.concatenate([moved_down(value).astype(BF16), here], -1)
                out[1, half, f] = jnp.concatenate([here, moved_up(value).astype(BF16)], -1)


def stacked(take, frames):
    return jnp.concatenate(
        [jnp.concatenate([take(f + a) for f in frames], 0) for a in range(3)], -1
    )


def activate(take, frames, skip, tiles, weight_ref, in_bias_ref, gain_ref, active, feature, evens=lambda: None):
    mid = gain_ref.shape[0]
    in_bias = in_bias_ref[...].reshape(1, mid)
    half_gain = gain_ref[...].reshape(1, mid) * 0.5
    me = position()
    top = (me > 0).astype(F32)
    bottom = (me < tiles - 1).astype(F32)
    for parity in range(2):
        if parity == 1:
            evens()
        weight = weight_ref[parity].reshape(-1, 2 * mid)
        for half in range(2):
            left = stacked(lambda f: take(parity, half, f), frames)
            wide = left.shape[0] // len(frames)
            summed = dot(left, weight)
            for near in range(2):
                row = half * 2 + near
                rounded = (summed[:, near * mid : (near + 1) * mid] + in_bias).astype(BF16)
                if row in (1, 2):
                    feature[row - 1, parity] = rounded[skip * wide :].reshape(-1, wide, mid)
                value = rounded.astype(F32)
                mean = jnp.mean(value * value, axis=-1, keepdims=True)
                scale = lax.rsqrt(mean + 1e-06)
                if row == 0:
                    scale = scale * top
                if row == 3:
                    scale = scale * bottom
                h = value * scale * half_gain
                active[row, parity, frames.start : frames.stop] = (
                    (h + h * jnp.tanh(h)).astype(BF16).reshape(len(frames), wide, mid)
                )


def transform(active, f, u, spectrum, parts=range(4)):
    def over_rows(parity):
        r = [active[row, parity, f].astype(F32) for row in ((0, 2), (1, 2), (2, 1), (1, 3))[u]]
        return r[0] + r[1] if u == 1 else r[0] - r[1]

    even = over_rows(0) if set(parts) - {0} else None
    odd = over_rows(1) if set(parts) - {3} else None
    for v in parts:
        if v == 0:
            value = moved_down(odd) - odd
        elif v == 1:
            value = even + odd
        elif v == 2:
            value = odd - even
        else:
            value = even - moved_up(even)
        spectrum[u * 4 + v][f] = value.astype(BF16)


def front_kernel(
    own_ref, token_weight_ref, in_bias_ref, gain_ref, windows_ref, feature_ref, spectrum_ref, active
):
    windows(own_ref, 0, windows_ref)
    activate(
        lambda parity, half, f: windows_ref[parity, half, f],
        range(windows_ref.shape[2] - 2),
        0,
        own_ref.shape[0],
        token_weight_ref,
        in_bias_ref,
        gain_ref,
        active,
        feature_ref,
    )
    parts = [spectrum_ref.at[at] for at in range(16)]
    for u in range(4):
        for f in range(active.shape[2]):
            transform(active, f, u, parts)


def block_kernel(
    previous_ref,
    windows_ref,
    late_feature_ref,
    late_spectrum_ref,
    token_weight_ref,
    in_bias_ref,
    gain_ref,
    mixed_0_ref,
    mixed_1_ref,
    mixed_2_ref,
    mid_bias_ref,
    out_ref,
    early_windows,
    active,
    feature,
    spectrum,
    lines,
    rounded,
    sent,
):
    tiles = previous_ref.shape[0]
    frames, rows, _, mid = out_ref.shape
    held = early_windows.shape[2]
    early = spectrum[0].shape[0]
    late = frames - late_feature_ref.shape[2]
    wide = spectrum[0].shape[1]

    def run(start):
        if start == 0:
            windows(previous_ref, 0, early_windows)

        def window(parity, half, f):
            if f >= held:
                return windows_ref[parity, half, f - held]
            if start:
                return jnp.zeros(early_windows.shape[3:], BF16)
            return early_windows[parity, half, f]

        activate(
            window,
            range(start, early),
            2 - start,
            tiles,
            token_weight_ref,
            in_bias_ref,
            gain_ref,
            active,
            feature,
            lambda: [
                transform(active, f, u, spectrum, (3,)) for u in range(4) for f in range(start, early)
            ],
        )

        def back(m0, m1, m2, m3):
            return m0 + 0.5 * (m1 + m2), 0.5 * (m1 - m2) - m3

        def product(at):
            def take(f):
                if f < start:
                    return jnp.zeros((wide, mid), BF16)
                return spectrum[at][f] if f < early else late_spectrum_ref[at, f - early]

            right = jnp.concatenate([ref[at] for ref in (mixed_0_ref, mixed_1_ref, mixed_2_ref)], 0)
            left = stacked(take, range(frames))
            return lax.dot_general(right, left, (((0,), (1,)), ((), ())), preferred_element_type=F32)

        mid_bias = mid_bias_ref[...].reshape(1, mid)

        def finish(row, totals):
            for parity in range(2):
                total = (totals[parity].T + mid_bias).reshape(frames, wide, mid)
                for f in range(frames):
                    held_feature = (
                        feature[row, parity, f] if f < late else late_feature_ref[row, parity, f - late]
                    )
                    value = total[f] + held_feature.astype(F32)
                    for lane in range(mid // LANES):
                        lines[f, lane, pl.ds(parity, wide, stride=2), :] = value[
                            :, lane * LANES : (lane + 1) * LANES
                        ]
            for f in range(frames):
                for lane in range(mid // LANES):
                    rounded[row, f, :, lane * LANES : (lane + 1) * LANES] = lines[
                        f, lane, : 2 * wide
                    ].astype(BF16)
            copy = pltpu.make_async_copy(rounded.at[row], out_ref.at[:, row], sent.at[row])
            copy.start()
            return copy

        def chores(u):
            return [functools.partial(transform, active, f, u, spectrum, (0, 1, 2)) for f in range(start, early)]

        last = []
        todo = chores(0) + chores(1)
        for u in range(4):
            last.append(product(u * 4 + 3))
            for chore in todo[u::4]:
                chore()
        sums = []
        copies = []
        for u in range(4):
            todo = chores(u + 2) if u < 2 else []
            parts = []
            for v in range(3):
                parts.append(product(u * 4 + v))
                for chore in todo[v::3]:
                    chore()
            sums.append(back(*parts, last[u]))
            if u == 2:
                totals = [sums[0][p] + 0.5 * (sums[1][p] + sums[2][p]) for p in range(2)]
                copies.append(finish(0, totals))
        totals = [0.5 * (sums[1][p] - sums[2][p]) - sums[3][p] for p in range(2)]
        copies.append(finish(1, totals))
        for copy in copies:
            copy.wait()

    pl.when(lax.axis_index("tm") > 0)(lambda: run(0))
    pl.when(lax.axis_index("tm") == 0)(lambda: run(2))


def limited(mebibytes):
    return pltpu.CompilerParams(vmem_limit_bytes=mebibytes * 2**20)


def after(value, *others):
    return lax.optimization_barrier((value, *others))[0]


def fast(value):
    return pltpu.with_memory_space_constraint(value, pltpu.VMEM)


def far(value):
    return pltpu.with_memory_space_constraint(value, pltpu.HBM)


def exchanged(keep, send, axis, beside):
    count = lax.axis_size(axis)
    size = count // 2
    while True:
        got = lax.ppermute(send, axis, [(one, one ^ size) for one in range(count)])
        done = beside(send)
        if size == 1:
            return after(jnp.concatenate([keep, got], 0), *done)
        size //= 2
        half = jax.ShapeDtypeStruct((2 * keep.shape[0], size + 2, *keep.shape[2:]), keep.dtype)
        keep, send = pl.pallas_call(
            halves_kernel, out_shape=(half, half), compiler_params=limited(2), name="halves"
        )(keep, got)
        send = after(send, *done)


def shifted(value, axis):
    count = lax.axis_size(axis)
    return lax.ppermute(value, axis, [(at, (at + 1) % count) for at in range(count)])


def per_device(
    latent_tokens, conv_in_weight, conv_in_bias, norm_gain, conv_mid_weight, conv_mid_bias
):
    frames, token_rows, cols, width = latent_tokens.shape
    tiles = lax.axis_size("space")
    assert token_rows == tiles and tiles & (tiles - 1) == 0 and frames == 4
    mid = conv_mid_weight.shape[-1]
    wide = tiles * cols
    line = (frames // 2, cols, 2 * width)

    half = jax.ShapeDtypeStruct((1, tiles // 2 + 2) + line, BF16)
    keep, send = pl.pallas_call(
        chunks_kernel,
        out_shape=(half, half),
        in_specs=[pl.BlockSpec(memory_space=pltpu.HBM)],
        scratch_shapes=[
            pltpu.VMEM(latent_tokens.shape, BF16),
            pltpu.SemaphoreType.DMA((frames,)),
        ],
        compiler_params=limited(2),
        name="chunks",
    )(far(latent_tokens))
    mixed = []

    def beside(value):
        time = len(mixed)
        if time == 3:
            return ()
        weight = far(after(conv_mid_weight, value))
        mixed.append(
            pl.pallas_call(
                functools.partial(mixed_kernel, time),
                out_shape=pltpu.VMEM((16, mid, mid), BF16),
                in_specs=[pl.BlockSpec(memory_space=pltpu.HBM)],
                scratch_shapes=[pltpu.VMEM((3, 3, mid, mid), BF16), pltpu.SemaphoreType.DMA((4,))],
                cost_estimate=pl.CostEstimate(
                    flops=0, bytes_accessed=50 * mid * mid, transcendentals=0
                ),
                compiler_params=limited(6),
                name="mixed",
            )(weight)
        )
        if time < 2:
            return mixed[-1:]
        token_weight.append(
            pl.pallas_call(
                token_weight_kernel,
                out_shape=pltpu.VMEM((2, 3, 4 * width, 2 * mid), BF16),
                cost_estimate=pl.CostEstimate(
                    flops=0, bytes_accessed=4 * 2**20, transcendentals=0
                ),
                compiler_params=limited(4),
                name="token_weight",
            )(conv_in_weight)
        )
        return mixed[-1:] + token_weight

    token_weight = []
    own = exchanged(keep, send, "space", beside)
    while len(mixed) < 3:
        beside(own)
    previous = shifted(own, "tm")

    late = 2
    early = frames + 2 - late
    windows_shape = (2, 2, frames, wide, 4 * width)
    own_windows, late_feature, late_spectrum = pl.pallas_call(
        front_kernel,
        out_shape=(
            pltpu.VMEM(windows_shape, BF16),
            pltpu.VMEM((2, 2, late, wide, mid), BF16),
            pltpu.VMEM((16, late, wide, mid), BF16),
        ),
        scratch_shapes=[pltpu.VMEM((4, 2, late, wide, mid), BF16)],
        cost_estimate=pl.CostEstimate(
            flops=0, bytes_accessed=50 * mid * mid, transcendentals=0
        ),
        compiler_params=limited(8),
        name="front",
    )(own, fast(token_weight[0]), conv_in_bias, norm_gain)

    return pl.pallas_call(
        block_kernel,
        out_shape=jax.ShapeDtypeStruct((frames, 2, 2 * wide, mid), BF16),
        out_specs=pl.BlockSpec(memory_space=pltpu.HBM),
        scratch_shapes=[
            pltpu.VMEM(windows_shape, BF16),
            pltpu.VMEM((4, 2, early, wide, mid), BF16),
            pltpu.VMEM((2, 2, frames - late, wide, mid), BF16),
            [pltpu.VMEM((early, wide, mid), BF16) for _ in range(16)],
            pltpu.VMEM((frames, mid // LANES, 2 * wide + SUBLANES, LANES), F32),
            pltpu.VMEM((2, frames, 2 * wide, mid), BF16),
            pltpu.SemaphoreType.DMA((2,)),
        ],
        compiler_params=limited(24),
        name="block",
    )(
        previous,
        fast(own_windows),
        fast(late_feature),
        fast(late_spectrum),
        fast(token_weight[0]),
        conv_in_bias,
        norm_gain,
        *[fast(value) for value in mixed],
        conv_mid_bias,
    )


def solution(mesh):
    return jax.shard_map(
        per_device,
        mesh=mesh,
        in_specs=(P("tm", None, "space", None), P(), P(), P(), P(), P()),
        out_specs=P("tm", "space", None, None),
        check_vma=False,
    )
```
